256 devices in a mesh: ctx: 64 (over x, z, core), tp: 4 (over y).
Axes of the slice: x: 4, y: 4, z: 8, core: 2. Of those that a mesh axis runs over, the one named last changes fastest.
Arguments:
- x_stream: bfloat16 [8192, 8192], P('ctx', 'tp'), may hold values from -6 to 6
- z_stream: bfloat16 [8192, 8192], P('ctx', 'tp'), may hold values from -6 to 6
- conv_kernel: float32 [4, 8192], P(None, 'tp'), may hold values from -3 to 3
- conv_bias: float32 [8192], P('tp'), may hold values from -0.5 to 0.5
- delta_down: bfloat16 [8192, 256], P('tp'), may hold values from -0.0625 to 0.0625
- state_proj: bfloat16 [32, 8192], P(None, 'tp'), may hold values from -0.0625 to 0.0625
- delta_up: bfloat16 [256, 8192], P(None, 'tp'), may hold values from -0.375 to 0.375
- delta_bias: float32 [8192], P('tp'), may hold values from -4.6 to -3
- log_decay: float32 [16, 8192], P(None, 'tp'), may hold values from -6 to 0
- skip_gain: float32 [8192], P('tp'), may hold values from 0.5 to 1.5
- queries: bfloat16 [8192, 4096], P('ctx', 'tp'), may hold values from -40 to 40
- key_heads: bfloat16 [8192, 1024], P('ctx', 'tp'), may hold values from -6 to 6
- values: bfloat16 [8192, 1024], P('ctx', 'tp'), may hold values from -24 to 24
- out_proj: bfloat16 [4096, 4096], P('tp', 'ctx'), may hold values from -0.09375 to 0.09375
- residual: bfloat16 [8192, 4096], P('ctx', 'tp'), may hold values from -1.5 to 1.5
Outputs:
- mixer_out: bfloat16 [8192, 8192], P('ctx', 'tp')
- block_out: bfloat16 [8192, 4096], P('ctx', 'tp')
The draws below stay inside these ranges and needn't reach their ends.
All inputs are finite; a program needn't handle non-finite values.
Results may differ from the reference program's by a relative error of at most 0.02.
Values may be sent and summed in bfloat16 or wider, within the bound.
A program may use at most 192 MiB of HBM per device.

```python
import math
import jax
import jax.numpy as jnp
from jax import lax

D = 4096
INNER = 8192
NS = 16
CONV = 4
DTR = 256
QH = 32
KVH = 8
HD = 128
SEQ = 8192


def base_fields(key):
    normal_part = jax.random.normal(jax.random.fold_in(key, 101), (SEQ, KVH * HD), jnp.float32)
    return normal_part


def draw_key_heads(key, part):
    normal_part = base_fields(key)
    return jnp.clip(normal_part, -6.0, 6.0).astype(jnp.bfloat16)


def draw_queries(key, part):
    key = jax.random.fold_in(key, 2)
    return jnp.clip(jax.random.normal(key, (SEQ, QH * HD), jnp.float32), -6.0, 6.0).astype(jnp.bfloat16)


def block_scale(rng, dims, split, least, largest):
    factor_of = 1.0
    for position, blocks in split:
        draws = jax.random.uniform(jax.random.fold_in(jax.random.fold_in(rng, 6), position), (blocks,), jnp.float32, least / len(split), largest / len(split))
        factor_of = factor_of * jnp.repeat(jnp.exp(draws), dims[position] // blocks).reshape((-1,) + (1,) * (len(dims) - 1 - position))
    return factor_of


def noise(key, extent, scale, limit, split=(), kind=jnp.bfloat16):
    drawn = jax.random.normal(key, extent, jnp.float32) * scale
    if len(split) > 0:
        drawn = block_scale(key, extent, split, -0.22, 0.18) * drawn
    return jnp.clip(drawn, min=-limit, max=limit).astype(kind)


def setup_inputs(seed: int = 0) -> dict:
    streams_of = jax.random.split(jax.random.key(seed), 16)
    x_stream = noise(streams_of[0], (SEQ, INNER), 1.0, 6.0, ((0, 64), (1, 4)))
    z_stream = noise(streams_of[1], (SEQ, INNER), 1.0, 6.0, ((0, 64), (1, 4)))
    conv_kernel = noise(streams_of[2], (CONV, INNER), CONV ** -0.5, 3.0, ((1, 4),), jnp.float32)
    conv_bias = jnp.clip(jax.random.uniform(streams_of[3], (INNER,), jnp.float32, -0.5, 0.5) * block_scale(streams_of[3], (INNER,), ((0, 4),), -0.4, 0.0), -0.5, 0.5)
    delta_down = noise(streams_of[4], (INNER, DTR), INNER ** -0.5, 0.0625, ((0, 4),))
    state_proj = noise(streams_of[5], (2 * NS, INNER), INNER ** -0.5, 0.0625, ((1, 4),))
    delta_up = noise(streams_of[6], (DTR, INNER), DTR ** -0.5, 0.375, ((1, 4),))
    delta_bias = jnp.clip(-4.6 + 1.5999999 * jax.random.uniform(streams_of[7], (INNER,), jnp.float32) ** block_scale(streams_of[7], (INNER,), ((0, 4),), -0.2, 0.2), -4.6, -3.0)
    log_decay = jnp.clip(-6.0 + 6.0 * jax.random.uniform(streams_of[8], (NS, INNER), jnp.float32) ** block_scale(streams_of[8], (NS, INNER), ((1, 4),), -0.2, 0.2), -6.0, 0.0)
    skip_gain = jnp.clip(0.5 + 1.0 * jax.random.uniform(streams_of[9], (INNER,), jnp.float32) ** block_scale(streams_of[9], (INNER,), ((0, 4),), -0.2, 0.2), 0.5, 1.5)
    queries = draw_queries(jax.random.fold_in(streams_of[15], 71), 0)
    key_heads = draw_key_heads(jax.random.fold_in(streams_of[15], 71), 0)
    values = noise(streams_of[12], (SEQ, KVH * HD), 4.0, 24.0, ((0, 64), (1, 4)))
    out_proj = noise(streams_of[13], (QH * HD, D), (QH * HD) ** -0.5, 0.09375, ((0, 4), (1, 64)))
    residual = noise(streams_of[14], (SEQ, D), 0.25, 1.5, ((0, 64), (1, 4)))
    return {"x_stream": x_stream, "z_stream": z_stream, "conv_kernel": conv_kernel, "conv_bias": conv_bias, "delta_down": delta_down, "state_proj": state_proj, "delta_up": delta_up, "delta_bias": delta_bias, "log_decay": log_decay, "skip_gain": skip_gain, "queries": queries, "key_heads": key_heads, "values": values, "out_proj": out_proj, "residual": residual}


def attend_block(query_tile_rows, block_start, key_heads, values):
    inverse_scale_factor = 1.0 / math.sqrt(HD)
    key_projected = key_heads.reshape(SEQ, KVH, HD).astype(jnp.float32)
    value_projected = values.reshape(SEQ, KVH, HD).astype(jnp.float32)
    logit_scores = jnp.einsum('luqf,euf->uqle', query_tile_rows.astype(jnp.float32), key_projected) * inverse_scale_factor
    query_pos = block_start + jnp.arange(query_tile_rows.shape[0], dtype=jnp.int32)
    causal = jnp.arange(SEQ, dtype=jnp.int32)[None, :] <= query_pos[:, None]
    logit_scores = jnp.where(causal, logit_scores, -1e+30)
    peak = lax.optimization_barrier(jnp.max(logit_scores, axis=-1, keepdims=True))
    attention_probabilities = jnp.where(causal, jnp.exp(logit_scores - peak), 0.0)
    summed = lax.optimization_barrier(jnp.sum(attention_probabilities, axis=-1))
    softmax_weights = lax.optimization_barrier(attention_probabilities.astype(jnp.bfloat16)).astype(jnp.float32)
    attention_mixed = jnp.einsum('vemi,iva->mvea', softmax_weights, value_projected)
    attention_mixed = attention_mixed / jnp.transpose(summed, (2, 0, 1))[..., None]
    return attention_mixed.astype(jnp.bfloat16).reshape(query_tile_rows.shape[0], QH * HD)

def reference(x_stream, z_stream, conv_kernel, conv_bias, delta_down, state_proj, delta_up, delta_bias, log_decay, skip_gain, queries, key_heads, values, out_proj, residual):
    leading = jnp.zeros((CONV - 1, INNER), jnp.float32)
    padded = jnp.concatenate([leading, x_stream.astype(jnp.float32)], axis=0)
    convolved = conv_bias[None, :]
    for offset in range(CONV):
        convolved = convolved + conv_kernel[offset][None, :] * padded[offset:offset + SEQ]
    inner_act = lax.optimization_barrier(jax.nn.silu(convolved).astype(jnp.bfloat16))
    delta_low = jnp.dot(inner_act, delta_down, preferred_element_type=jnp.float32).astype(jnp.bfloat16)
    gates = jnp.dot(state_proj, inner_act.T, preferred_element_type=jnp.float32)
    step_size = jax.nn.softplus(jnp.dot(delta_low, delta_up, preferred_element_type=jnp.float32) + delta_bias[None, :])
    decay_rate = -jnp.exp(log_decay)
    act_float = inner_act.astype(jnp.float32)

    def advance(carried, inputs):
        step_row, act_row, in_gate, out_gate = inputs
        carried = jnp.exp(decay_rate * step_row[None, :]) * carried + in_gate[:, None] * (step_row * act_row)[None, :]
        return (carried, lax.optimization_barrier(jnp.sum(out_gate[:, None] * carried, axis=0)))
    _, scanned = lax.scan(advance, jnp.zeros((NS, INNER), jnp.float32), (step_size, act_float, gates[:NS].T, gates[NS:].T))
    mixer_out = ((scanned + skip_gain[None, :] * act_float) * jax.nn.silu(z_stream.astype(jnp.float32))).astype(jnp.bfloat16)
    query_blocks = queries.reshape(SEQ // 128, 128, KVH, QH // KVH, HD)
    block_starts = jnp.arange(SEQ // 128, dtype=jnp.int32) * 128
    attended = lax.map(lambda pair: attend_block(pair[0], pair[1], key_heads, values), (query_blocks, block_starts))
    attended = attended.reshape(SEQ, QH * HD)
    projected = jnp.dot(attended, out_proj, preferred_element_type=jnp.float32)
    block_out = (residual.astype(jnp.float32) + projected).astype(jnp.bfloat16)
    return (mixer_out, block_out)
```

```python
import math

import jax
import jax.numpy as jnp
from jax import lax
from jax.experimental import pallas as pl
from jax.experimental.pallas import tpu as pltpu
from jax.sharding import PartitionSpec as P

HD = 128
BF = jnp.bfloat16
F32 = jnp.float32
MESH = pl.DeviceIdType.MESH
NS = 16
LOG2E = math.log2(math.e)
SCALE = math.log2(math.e) / math.sqrt(HD)


def at(ctx, tp):
    return {"ctx": ctx, "tp": tp}


def ctx_of(x, z, core):
    return (x * 8 + z) * 2 + core


def ring_position(x, z, core):
    first = 4 * z + (x + z) % 4
    turn = (z + 5 * x) % 8
    second = 4 * (x + 4 * (turn // 4)) + turn % 4
    return (1 - core) * first + core * second


def ring_chip(position, core):
    major = position // 4
    minor = position % 4
    x = (1 - core) * ((minor + 3 * major) % 4) + core * (major % 4)
    z = (1 - core) * major + core * ((3 * major + minor) % 8)
    return x, z


def attn_kernel(
    q_ref, k_ref, v_ref, wt_ref, res_ref, out_ref,
    qts, vts, qt, kbuf, vtbuf, wbuf, m_ref, l_ref, acc, att, stage, landed, out_t,
    pair_send, pair_recv, ring_send, ring_recv, y_send, y_recv,
):
    me = lax.axis_index("ctx")
    y = lax.axis_index("tp")
    core = me % 2
    other = 1 - core
    z = (me // 2) % 8
    x = me // 16
    chip = me // 2
    partner = at(me + 1 - 2 * core, y)
    here = ring_position(x, z, core)
    xr, zr = ring_chip((here + 1) % 32, core)
    xl, zl = ring_chip((here + 31) % 32, core)
    right = at(ctx_of(xr, zr, core), y)
    left = at(ctx_of(xl, zl, core), y)

    barrier = pltpu.get_barrier_semaphore()
    for peer in (partner, right, left):
        pl.semaphore_signal(barrier, inc=1, device_id=peer, device_id_type=MESH)
    for step in (1, 2, 3):
        for r in range(2):
            pl.semaphore_signal(
                barrier, inc=1, device_id=at(chip * 2 + r, (y + step) % 4), device_id_type=MESH
            )
    for g in range(2):
        for h in range(4):
            head = q_ref[:, (g * 4 + h) * HD:(g * 4 + h + 1) * HD]
            qts[g, :, h * HD:(h + 1) * HD] = head.astype(F32).T.astype(BF)
    vts[...] = v_ref[...].astype(F32).T.astype(BF)
    pl.semaphore_wait(barrier, 9)

    own_rows = pl.ds(pl.multiple_of(core * 128, 128), 128)
    other_rows = pl.ds(pl.multiple_of(other * 128, 128), 128)
    own_cols = pl.ds(pl.multiple_of(core * 512, 512), 512)

    def pair_copy(src, dst, k):
        return pltpu.make_async_remote_copy(
            src_ref=src, dst_ref=dst, send_sem=pair_send.at[k], recv_sem=pair_recv.at[k],
            device_id=partner, device_id_type=MESH,
        )

    swaps = (
        pair_copy(k_ref.at[:, other_rows], kbuf.at[0, own_rows, :], 0),
        pair_copy(vts.at[other_rows, :], vtbuf.at[0, :, own_rows], 1),
        pair_copy(qts.at[other], qt.at[:, own_cols], 2),
    )
    for swap in swaps:
        swap.start()
    kbuf[0, own_rows, :] = k_ref[:, own_rows]
    vtbuf[0, :, own_rows] = vts[own_rows, :]
    qt[:, own_cols] = qts[core]
    wbuf[0] = wt_ref[...]
    m_ref[...] = jnp.full_like(m_ref, -1e30)
    l_ref[...] = jnp.zeros_like(l_ref)
    acc[...] = jnp.zeros_like(acc)
    bufs = (kbuf, vtbuf, wbuf)

    def ring_copy(kind, src, dst, peer):
        buf = bufs[kind]
        return pltpu.make_async_remote_copy(
            src_ref=buf.at[src], dst_ref=buf.at[dst],
            send_sem=ring_send.at[kind, dst], recv_sem=ring_recv.at[kind, dst],
            device_id=peer, device_id_type=MESH,
        )

    for kind in (0, 1):
        swaps[kind].wait()
        ring_copy(kind, 0, 1, right).start()
        ring_copy(kind, 0, 2, left).start()
    ring_copy(2, 0, 1, right).start()
    ring_copy(2, 0, 2, left).start()
    swaps[2].wait()

    def attend(slot, masked):
        for j in range(4):
            cols = pl.ds(j * 256, 256)
            s = jnp.dot(kbuf[slot], qt[:, cols], preferred_element_type=F32) * SCALE
            if masked:
                key = lax.broadcasted_iota(jnp.int32, (256, 256), 0)
                row = lax.broadcasted_iota(jnp.int32, (256, 256), 1) % 128 + (j // 2) * 128
                s = jnp.where(key <= row, s, -1e30)
            m_old = m_ref[:, cols]
            m_new = jnp.maximum(m_old, jnp.max(s, axis=0, keepdims=True))
            p = jnp.exp2(s - m_new)
            alpha = jnp.exp2(m_old - m_new)
            m_ref[:, cols] = m_new
            l_ref[:, cols] = l_ref[:, cols] * alpha + jnp.sum(p, axis=0, keepdims=True)
            acc[:, cols] = acc[:, cols] * alpha + jnp.dot(
                vtbuf[slot], p.astype(BF), preferred_element_type=F32
            )

    attend(0, True)

    def origin(slot_step, sign):
        return ring_chip((here + 32 - sign * slot_step) % 32, core)

    def step(s, _):
        plus, minus = 2 * s - 1, 2 * s
        for kind in (0, 1):
            ring_copy(kind, 0, plus, right).wait_recv()

            @pl.when(s < 16)
            def _():
                ring_copy(kind, plus, plus + 2, right).start()

                ring_copy(kind, 0, minus, left).wait_recv()

            @pl.when(s < 15)
            def _():
                ring_copy(kind, minus, minus + 2, left).start()

        xo, zo = origin(s, 1)

        @pl.when(xo * 8 + zo < chip)
        def _():
            attend(plus, False)

        xo, zo = origin(s, -1)

        @pl.when((s < 16) & (xo * 8 + zo < chip))
        def _():
            attend(minus, False)

        ring_copy(2, 0, plus, right).wait_recv()

        @pl.when(s < 16)
        def _():
            ring_copy(2, plus, plus + 2, right).start()
            ring_copy(2, 0, minus, left).wait_recv()

        @pl.when(s < 15)
        def _():
            ring_copy(2, minus, minus + 2, left).start()

        return 0

    lax.fori_loop(1, 17, step, 0)

    inverse = 1.0 / l_ref[...]
    own_feats = pl.ds(pl.multiple_of(core * 512, 512), 512)
    att_own = []
    for h in range(4):
        pieces = []
        for r in range(2):
            cols = slice(r * 512 + h * 128, r * 512 + (h + 1) * 128)
            pieces.append((acc[:, cols] * inverse[:, cols]).astype(BF))
        att_own.append(jnp.concatenate(pieces, axis=1))
    att[own_feats, :] = jnp.concatenate(att_own, axis=0)
    swap = pair_copy(att.at[own_feats, :], att.at[own_feats, :], 3)
    swap.start()
    swap.wait()

    def project(slot, xo, zo):
        part = jnp.dot(wbuf[slot], att[...], preferred_element_type=F32).astype(BF)
        rows = pl.ds(pl.multiple_of(zo * 64, 64), 64)
        stage[xo, 0, rows, :] = part[:, :128]
        stage[xo, 1, rows, :] = part[:, 128:]

    project(0, x, z)

    def project_step(s, _):
        xo, zo = origin(s, 1)
        project(2 * s - 1, xo, zo)
        xo, zo = origin(s, -1)

        @pl.when(s < 16)
        def _():
            project(2 * s, xo, zo)

        return 0

    lax.fori_loop(1, 17, project_step, 0)

    def y_copy(gap, r):
        there = (y + gap) % 4
        k = gap * 2 + r
        return pltpu.make_async_remote_copy(
            src_ref=stage.at[there, r], dst_ref=landed.at[gap, core],
            send_sem=y_send.at[k], recv_sem=y_recv.at[gap, core],
            device_id=at(chip * 2 + r, there), device_id_type=MESH,
        )

    def y_arrival(gap, c):
        return pltpu.make_async_remote_copy(
            src_ref=stage.at[0, 0], dst_ref=landed.at[gap, c],
            send_sem=y_send.at[0], recv_sem=y_recv.at[gap, c],
            device_id=partner, device_id_type=MESH,
        )

    for gap in (2, 1, 3):
        for r in range(2):
            y_copy(gap, r).start()
    swap = pltpu.make_async_remote_copy(
        src_ref=stage.at[y, other], dst_ref=landed.at[0, core],
        send_sem=y_send.at[0], recv_sem=y_recv.at[0, core],
        device_id=partner, device_id_type=MESH,
    )
    swap.start()
    landed[0, core] = stage[y, core]
    y_arrival(0, other).wait_recv()
    for gap in (1, 3, 2):
        for c in range(2):
            y_arrival(gap, c).wait_recv()
    total = landed[0].astype(F32)
    for gap in range(1, 4):
        total = total + landed[gap].astype(F32)
    for zo in range(8):
        for c in range(2):
            out_t[zo * 128 + c * 64:zo * 128 + c * 64 + 64, :] = total[c, zo * 64:zo * 64 + 64, :]
    for zo in range(8):
        cols = slice(zo * 128, (zo + 1) * 128)
        out_ref[:, cols] = (res_ref[:, cols].astype(F32) + out_t[cols, :].T).astype(BF)
    swap.wait_send()
    for gap in (1, 2, 3):
        for r in range(2):
            y_copy(gap, r).wait_send()

    def drain(s, _):
        for kind in range(3):
            ring_copy(kind, 0, 2 * s - 1, right).wait_send()

            @pl.when(s < 16)
            def _():
                ring_copy(kind, 0, 2 * s, left).wait_send()

        return 0

    lax.fori_loop(1, 17, drain, 0)


def attention(queries, key_heads, values, out_proj, residual):
    vmem = pl.BlockSpec(memory_space=pltpu.VMEM)
    return pl.pallas_call(
        attn_kernel,
        out_shape=jax.ShapeDtypeStruct(residual.shape, BF),
        in_specs=[vmem] * 5,
        out_specs=vmem,
        scratch_shapes=[
            pltpu.VMEM((2, 128, 512), BF),
            pltpu.VMEM((256, 128), BF),
            pltpu.VMEM((128, 1024), BF),
            pltpu.VMEM((32, 256, 128), BF),
            pltpu.VMEM((32, 128, 256), BF),
            pltpu.VMEM((32, 64, 1024), BF),
            pltpu.VMEM((1, 1024), F32),
            pltpu.VMEM((1, 1024), F32),
            pltpu.VMEM((128, 1024), F32),
            pltpu.VMEM((1024, 256), BF),
            pltpu.VMEM((4, 2, 512, 128), BF),
            pltpu.VMEM((4, 2, 512, 128), BF),
            pltpu.VMEM((1024, 128), F32),
            pltpu.SemaphoreType.DMA((4,)),
            pltpu.SemaphoreType.DMA((4,)),
            pltpu.SemaphoreType.DMA((3, 32)),
            pltpu.SemaphoreType.DMA((3, 32)),
            pltpu.SemaphoreType.DMA((8,)),
            pltpu.SemaphoreType.DMA((4, 2)),
        ],
        compiler_params=pltpu.CompilerParams(
            collective_id=0, has_side_effects=True, vmem_limit_bytes=48 * 1024 * 1024
        ),
    )(queries, key_heads, values, out_proj.T, residual)


def ssm_kernel(
    x_ref, z_ref, ck_ref, cb_ref, dd_ref, sp_ref, du_ref, db_ref, ld_ref, sg_ref, out_ref,
    rim, padded, act, dpart, gpart, dland, gland, gsum, gates, steps, inject, scanned, decay,
    ends, total, ends_in, total_in, before, shift, column, column_in, entry_out, entry,
    rim_send, rim_recv, tp_send, tp_recv, col_send, col_recv, x_send, x_recv, back_send, back_recv, local_sem,
):
    me = lax.axis_index("ctx")
    y = lax.axis_index("tp")
    x = me // 16
    k = me % 16
    after = at((me + 1) % 64, y)
    earlier = at((me + 63) % 64, y)

    def tp_peer(gap):
        return at(me, (y + gap) % 4)

    def col_peer(gap):
        return at(x * 16 + (k + gap) % 16, y)

    def x_peer(gap):
        return at(((x + gap) % 4) * 16 + k, y)

    barrier = pltpu.get_barrier_semaphore()

    def greet(peer):
        pl.semaphore_signal(barrier, inc=1, device_id=peer, device_id_type=MESH)

    greet(after)
    greet(earlier)
    for gap in (1, 2, 3):
        greet(tp_peer(gap))
        greet(x_peer(gap))
    for gap in range(1, 16):
        greet(col_peer(gap))
    padded[8:, :] = x_ref[...].astype(F32)
    pl.semaphore_wait(barrier, 23)

    def remote(src, dst, send, recv, peer):
        return pltpu.make_async_remote_copy(
            src_ref=src, dst_ref=dst, send_sem=send, recv_sem=recv, device_id=peer, device_id_type=MESH
        )

    rim_copy = remote(x_ref.at[pl.ds(112, 16), :], rim, rim_send.at[0], rim_recv.at[0], after)
    rim_copy.start()
    rate = -LOG2E * jnp.exp(ld_ref[...])
    for j in range(16):
        decay[pl.ds(j, 16, stride=16), :] = rate[:, j * 128:(j + 1) * 128]
    rim_copy.wait()
    padded[:8, :] = jnp.where(me > 0, rim[8:, :].astype(F32), 0.0)

    for c in range(8):
        cols = slice(c * 256, (c + 1) * 256)
        conv = cb_ref[:, cols]
        for tap in range(4):
            conv = conv + ck_ref[tap:tap + 1, cols] * padded[5 + tap:133 + tap, cols]
        act[:, cols] = (conv / (1.0 + jnp.exp(-conv))).astype(BF)
    dpart[...] = jnp.dot(act[...], dd_ref[...], preferred_element_type=F32).astype(BF)
    gpart[...] = lax.dot_general(
        sp_ref[...], act[...], (((1,), (1,)), ((), ())), preferred_element_type=F32
    )

    def tp_copies(gap):
        return (
            remote(dpart, dland.at[gap - 1], tp_send.at[0, gap], tp_recv.at[0, gap], tp_peer(gap)),
            remote(gpart, gland.at[gap - 1], tp_send.at[1, gap], tp_recv.at[1, gap], tp_peer(gap)),
        )

    for gap in (2, 1, 3):
        for copy in tp_copies(gap):
            copy.start()
    for gap in (1, 3, 2):
        for copy in tp_copies(gap):
            copy.wait()
    gsum[...] = gpart[...] + gland[0] + gland[1] + gland[2]
    to_scalars = pltpu.make_async_copy(gsum, gates, local_sem.at[0])
    to_scalars.start()
    low = (
        dpart[...].astype(F32) + dland[0].astype(F32) + dland[1].astype(F32) + dland[2].astype(F32)
    ).astype(BF)
    for c in range(8):
        cols = slice(c * 256, (c + 1) * 256)
        raw = jnp.dot(low, du_ref[:, cols], preferred_element_type=F32) + db_ref[:, cols]
        size = jnp.maximum(raw, 0.0) + jnp.log1p(jnp.exp(-jnp.abs(raw)))
        drive = size * act[:, cols].astype(F32)
        for half in range(2):
            j = c * 2 + half
            steps[pl.ds(j, 128, stride=16), :] = size[:, half * 128:(half + 1) * 128]
            inject[pl.ds(j, 128, stride=16), :] = drive[:, half * 128:(half + 1) * 128]
    to_scalars.wait()

    def rows_of(t):
        return pl.ds(pl.multiple_of(t * 16, 16), 16)

    for half in range(2):
        base = half * 8
        rates = [decay[(base + n) * 16:(base + n + 1) * 16, :] for n in range(8)]

        def advance(t, carried):
            size = steps[rows_of(t), :]
            drive = inject[rows_of(t), :]
            out = [
                jnp.exp2(rates[n] * size) * carried[n] + gates[base + n, t] * drive
                for n in range(8)
            ]
            return tuple(out) + (carried[8] + size,)

        zero = jnp.zeros((16, 128), F32)
        last = lax.fori_loop(0, 128, advance, (zero,) * 9, unroll=2)
        for n in range(8):
            ends[base + n] = last[n]
        if half == 0:
            total[...] = last[8]

    def col_copies(gap):
        return (
            remote(ends.at[(k + gap) % 16], ends_in.at[gap], col_send.at[0, gap], col_recv.at[0, gap], col_peer(gap)),
            remote(total, total_in.at[gap], col_send.at[1, gap], col_recv.at[1, gap], col_peer(gap)),
        )

    def col_start(gap, _):
        for copy in col_copies(gap):
            copy.start()
        return 0

    def col_wait(gap, _):
        for copy in col_copies(gap):
            copy.wait()
        return 0

    lax.fori_loop(1, 16, col_start, 0)
    ends_in[0] = ends[k]
    total_in[0] = total[...]
    my_rate = decay[rows_of(k), :]
    lax.fori_loop(1, 16, col_wait, 0)

    def chain(j, carried):
        state, sizes = carried
        before[j] = state
        shift[j] = sizes
        slot = (k + 16 - j) % 16
        size = total_in[slot]
        return (jnp.exp2(my_rate * size) * state + ends_in[slot], sizes + size)

    zero = jnp.zeros((16, 128), F32)
    state, sizes = lax.fori_loop(0, 16, chain, (zero, zero))
    column[0] = state
    column[1] = sizes

    def x_copy(gap):
        return remote(column, column_in.at[gap - 1], x_send.at[gap], x_recv.at[gap], x_peer(gap))

    for gap in (2, 1, 3):
        x_copy(gap).start()
    for gap in (1, 3, 2):
        x_copy(gap).wait()
    incoming = zero
    for xs in range(3):
        slot = jnp.minimum((x + 3 - xs) % 4, 2)
        ahead = jnp.exp2(my_rate * column_in[slot, 1]) * incoming + column_in[slot, 0]
        incoming = jnp.where(xs < x, ahead, incoming)

    def finish(j, _):
        entry_out[j] = before[j] + jnp.exp2(my_rate * shift[j]) * incoming
        return 0

    lax.fori_loop(0, 16, finish, 0)

    def back_copy(gap):
        return remote(
            entry_out.at[(k + gap) % 16], entry.at[k], back_send.at[gap], back_recv.at[gap], col_peer(gap)
        )

    def back_arrival(gap):
        return remote(
            entry_out.at[(k + gap) % 16], entry.at[(k + 16 - gap) % 16], back_send.at[gap], back_recv.at[gap], col_peer(gap)
        )

    def back_start(gap, _):
        back_copy(gap).start()
        return 0

    def back_wait(gap, _):
        back_copy(gap).wait_send()
        back_arrival(gap).wait_recv()
        return 0

    lax.fori_loop(1, 16, back_start, 0)
    entry[k] = entry_out[k]
    lax.fori_loop(1, 16, back_wait, 0)

    for half in range(2):
        base = half * 8
        rates = [decay[(base + n) * 16:(base + n + 1) * 16, :] for n in range(8)]

        def advance(t, carried):
            size = steps[rows_of(t), :]
            drive = inject[rows_of(t), :]
            out = []
            mixed = scanned[rows_of(t), :] if half else None
            for n in range(8):
                state = jnp.exp2(rates[n] * size) * carried[n] + gates[base + n, t] * drive
                term = gates[NS + base + n, t] * state
                mixed = term if mixed is None else mixed + term
                out.append(state)
            scanned[rows_of(t), :] = mixed
            return tuple(out)

        lax.fori_loop(0, 128, advance, tuple(entry[base + n] for n in range(8)), unroll=2)

    for j in range(16):
        cols = slice(j * 128, (j + 1) * 128)
        gate = z_ref[:, cols].astype(F32)
        mixed = scanned[pl.ds(j, 128, stride=16), :] + sg_ref[:, cols] * act[:, cols].astype(F32)
        out_ref[:, cols] = (mixed * (gate / (1.0 + jnp.exp(-gate)))).astype(BF)


def recurrence(
    x_stream, z_stream, conv_kernel, conv_bias, delta_down, state_proj, delta_up, delta_bias, log_decay, skip_gain
):
    vmem = pl.BlockSpec(memory_space=pltpu.VMEM)
    dma = pltpu.SemaphoreType.DMA
    return pl.pallas_call(
        ssm_kernel,
        out_shape=jax.ShapeDtypeStruct(x_stream.shape, BF),
        in_specs=[vmem] * 10,
        out_specs=vmem,
        scratch_shapes=[
            pltpu.VMEM((16, 2048), BF),
            pltpu.VMEM((136, 2048), F32),
            pltpu.VMEM((128, 2048), BF),
            pltpu.VMEM((128, 256), BF),
            pltpu.VMEM((32, 128), F32),
            pltpu.VMEM((3, 128, 256), BF),
            pltpu.VMEM((3, 32, 128), F32),
            pltpu.VMEM((32, 128), F32),
            pltpu.SMEM((32, 128), F32),
            pltpu.VMEM((2048, 128), F32),
            pltpu.VMEM((2048, 128), F32),
            pltpu.VMEM((2048, 128), F32),
            pltpu.VMEM((256, 128), F32),
            pltpu.VMEM((16, 16, 128), F32),
            pltpu.VMEM((16, 128), F32),
            pltpu.VMEM((16, 16, 128), F32),
            pltpu.VMEM((16, 16, 128), F32),
            pltpu.VMEM((16, 16, 128), F32),
            pltpu.VMEM((16, 16, 128), F32),
            pltpu.VMEM((2, 16, 128), F32),
            pltpu.VMEM((3, 2, 16, 128), F32),
            pltpu.VMEM((16, 16, 128), F32),
            pltpu.VMEM((16, 16, 128), F32),
            dma((1,)), dma((1,)), dma((2, 4)), dma((2, 4)), dma((2, 16)), dma((2, 16)),
            dma((4,)), dma((4,)), dma((16,)), dma((16,)), dma((1,)),
        ],
        compiler_params=pltpu.CompilerParams(
            collective_id=1, has_side_effects=True, vmem_limit_bytes=48 * 1024 * 1024
        ),
    )(
        x_stream, z_stream, conv_kernel, conv_bias[None, :], delta_down, state_proj, delta_up,
        delta_bias[None, :], log_decay, skip_gain[None, :],
    )


def local(
    x_stream, z_stream, conv_kernel, conv_bias, delta_down, state_proj, delta_up, delta_bias,
    log_decay, skip_gain, queries, key_heads, values, out_proj, residual,
):
    mixer_out = recurrence(
        x_stream, z_stream, conv_kernel, conv_bias, delta_down, state_proj, delta_up, delta_bias,
        log_decay, skip_gain,
    )
    block_out = attention(queries, key_heads, values, out_proj, residual)
    return mixer_out, block_out


def solution(mesh):
    both = P("ctx", "tp")
    placed = (
        both, both, P(None, "tp"), P("tp"), P("tp", None), P(None, "tp"), P(None, "tp"), P("tp"),
        P(None, "tp"), P("tp"), both, both, both, P("tp", "ctx"), both,
    )
    return jax.shard_map(
        local, mesh=mesh, in_specs=placed, out_specs=(both, both), check_vma=False
    )
```

```python
import math

import jax
import jax.numpy as jnp
from jax import lax
from jax.experimental import pallas as pl
from jax.experimental.pallas import tpu as pltpu
from jax.sharding import PartitionSpec as P

HD = 128
NS = 16
BF = jnp.bfloat16
F32 = jnp.float32
MESH = pl.DeviceIdType.MESH
LOG2E = math.log2(math.e)
SCALE = LOG2E / math.sqrt(HD)
X_OFFSET = (0, 3, 1, 2)
GROUPS = ((0, 1), (1, 2), (3, 2), (5, 2), (7, 1))


def at(ctx, tp):
    return {"ctx": ctx, "tp": tp}


def remote(src, dst, send, recv, peer):
    return pltpu.make_async_remote_copy(
        src_ref=src, dst_ref=dst, send_sem=send, recv_sem=recv, device_id=peer, device_id_type=MESH
    )


def block_kernel(
    x_hbm, z_hbm, ck_hbm, cb_hbm, dd_hbm, sp_hbm, du_hbm, db_hbm, ld_hbm, sg_hbm,
    q_hbm, k_hbm, v_hbm, wt_hbm, res_hbm, mix_ref, out_ref,
    x_ref, z_ref, ck_ref, cb_ref, dd_ref, sp_ref, du_ref, db_ref, ld_ref, sg_ref,
    q_ref, k_ref, v_ref, res_ref,
    qts, vts, qt, kbuf, vtbuf, wbuf, m_ref, l_ref, acc, att, stage, landed, out_t,
    rim, padded, act, dpart, gpart, dland, gland, gsum, gates, steps, inject, scanned, decay,
    ends, total, ends_in, total_in, before, shift, column, column_in, entry_out, entry,
    load_sem, pair_send, pair_recv, kv_send, kv_recv, w_send, w_recv, half_send, half_recv,
    y_send, y_recv, rim_send, rim_recv, tp_send, tp_recv, col_send, col_recv, x_send, x_recv,
    back_send, back_recv,
):
    me = lax.axis_index("ctx")
    y = lax.axis_index("tp")
    core = me % 2
    other = 1 - core
    chip = me // 2
    z = chip % 8
    x = me // 16
    k = me % 16
    partner = at(me + 1 - 2 * core, y)
    after = at((me + 1) % 64, y)
    earlier = at((me + 63) % 64, y)
    right_z = at(x * 16 + ((z + 1) % 8) * 2 + core, y)
    left_z = at(x * 16 + ((z + 7) % 8) * 2 + core, y)
    right_x = at(((x + 1) % 4) * 16 + k, y)
    left_x = at(((x + 3) % 4) * 16 + k, y)

    def col_peer(gap):
        return at(x * 16 + (k + gap) % 16, y)

    def x_peer(gap):
        return at(((x + gap) % 4) * 16 + k, y)

    loads = {}
    pairs = (
        ("q", q_hbm, q_ref), ("k", k_hbm, k_ref), ("v", v_hbm, v_ref), ("w", wt_hbm, wbuf.at[0, 0]),
        ("x", x_hbm, x_ref), ("ck", ck_hbm, ck_ref), ("cb", cb_hbm, cb_ref), ("dd", dd_hbm, dd_ref),
        ("sp", sp_hbm, sp_ref), ("ld", ld_hbm, ld_ref), ("du", du_hbm, du_ref), ("db", db_hbm, db_ref),
        ("z", z_hbm, z_ref), ("sg", sg_hbm, sg_ref), ("res", res_hbm, res_ref),
    )
    for i, (name, src, dst) in enumerate(pairs):
        loads[name] = pltpu.make_async_copy(src, dst, load_sem.at[i])
        loads[name].start()

    barrier = pltpu.get_barrier_semaphore()

    def greet(peer):
        pl.semaphore_signal(barrier, inc=1, device_id=peer, device_id_type=MESH)

    greet(after)
    greet(earlier)
    for gap in (1, 2, 3):
        greet(x_peer(gap))
        for r in range(2):
            greet(at(chip * 2 + r, (y + gap) % 4))
    for gap in range(1, 16):
        greet(col_peer(gap))

    loads["q"].wait()
    for g in range(2):
        for h in range(4):
            head = q_ref[:, (g * 4 + h) * HD:(g * 4 + h + 1) * HD]
            qts[g, :, h * HD:(h + 1) * HD] = head.astype(F32).T.astype(BF)
    loads["k"].wait()
    loads["v"].wait()
    vts[...] = v_ref[...].astype(F32).T.astype(BF)
    loads["w"].wait()
    loads["x"].wait()
    pl.semaphore_wait(barrier, 26)

    own_rows = pl.ds(pl.multiple_of(core * 128, 128), 128)
    other_rows = pl.ds(pl.multiple_of(other * 128, 128), 128)
    own_cols = pl.ds(pl.multiple_of(core * 512, 512), 512)

    def pair_copy(src, dst, i):
        return remote(src, dst, pair_send.at[i], pair_recv.at[i], partner)

    swaps = (
        pair_copy(k_ref.at[:, other_rows], kbuf.at[0, 0, own_rows, :], 0),
        pair_copy(vts.at[other_rows, :], vtbuf.at[0, 0, :, own_rows], 1),
        pair_copy(qts.at[other], qt.at[:, own_cols], 2),
    )
    for swap in swaps:
        swap.start()
    rim_copy = remote(x_ref.at[pl.ds(112, 16), :], rim, rim_send.at[0], rim_recv.at[0], after)
    rim_copy.start()

    bufs = (kbuf, vtbuf)

    def kv_copy(kind, src, dst, peer):
        return remote(
            bufs[kind].at[src], bufs[kind].at[dst], kv_send.at[(kind, *dst)], kv_recv.at[(kind, *dst)], peer
        )

    def kv_arrived(kind, slot):
        kv_copy(kind, slot, slot, right_z).wait_recv()

    def spread_x(kind, zs):
        kv_copy(kind, (0, zs), (1, zs), right_x).start()
        kv_copy(kind, (0, zs), (2, zs), left_x).start()

    def w_copy(src, dst, peer):
        return remote(wbuf.at[src], wbuf.at[dst], w_send.at[dst], w_recv.at[dst], peer)

    def w_arrived(slot):
        w_copy(slot, slot, right_z).wait_recv()

    def half_copy(source, rows, i, peer):
        half = pl.ds(rows, 32)
        return remote(
            wbuf.at[0, source, half, :], wbuf.at[0, 3, half, :], half_send.at[i], half_recv.at[i], peer
        )

    def w_spread_z(xs):
        w_copy((0, xs), (1, xs), right_z).start()
        w_copy((0, xs), (2, xs), left_z).start()

    kbuf[0, 0, own_rows, :] = k_ref[:, own_rows]
    vtbuf[0, 0, :, own_rows] = vts[own_rows, :]
    qt[:, own_cols] = qts[core]
    for kind in (0, 1):
        swaps[kind].wait()
        kv_copy(kind, (0, 0), (0, 1), right_z).start()
        kv_copy(kind, (0, 0), (0, 2), left_z).start()
        spread_x(kind, 0)
    w_copy((0, 0), (0, 1), right_x).start()
    w_copy((0, 0), (0, 2), left_x).start()
    m_ref[...] = jnp.full_like(m_ref, -1e30)
    l_ref[...] = jnp.zeros_like(l_ref)
    acc[...] = jnp.zeros_like(acc)

    def kv_hop(h):
        for kind in (0, 1):
            if h < 4:
                kv_arrived(kind, (0, 2 * h - 1))
                if h < 3:
                    kv_copy(kind, (0, 2 * h - 1), (0, 2 * h + 1), right_z).start()
                elif kind == 0:
                    kv_copy(kind, (0, 5), (0, 7), right_z).start()
                spread_x(kind, 2 * h - 1)
                kv_arrived(kind, (0, 2 * h))
                if h < 3:
                    kv_copy(kind, (0, 2 * h), (0, 2 * h + 2), left_z).start()
                elif kind == 1:
                    kv_copy(kind, (0, 6), (0, 7), left_z).start()
                spread_x(kind, 2 * h)
            else:
                kv_arrived(kind, (0, 7))
                spread_x(kind, 7)

    loads["ck"].wait()
    loads["cb"].wait()
    padded[8:, :] = x_ref[...].astype(F32)
    rim_copy.wait()
    padded[:8, :] = jnp.where(me > 0, rim[8:, :].astype(F32), 0.0)
    for c in range(8):
        cols = slice(c * 256, (c + 1) * 256)
        conv = cb_ref[:, cols]
        for tap in range(4):
            conv = conv + ck_ref[tap:tap + 1, cols] * padded[5 + tap:133 + tap, cols]
        act[:, cols] = (conv / (1.0 + jnp.exp(-conv))).astype(BF)
    loads["dd"].wait()
    loads["sp"].wait()
    dpart[...] = jnp.dot(act[...], dd_ref[...], preferred_element_type=F32).astype(BF)
    gpart[...] = lax.dot_general(
        sp_ref[...], act[...], (((1,), (1,)), ((), ())), preferred_element_type=F32
    )

    def tp_copies(gap):
        peer = at(me, (y + gap) % 4)
        return (
            remote(dpart, dland.at[gap - 1], tp_send.at[0, gap], tp_recv.at[0, gap], peer),
            remote(gpart, gland.at[gap - 1], tp_send.at[1, gap], tp_recv.at[1, gap], peer),
        )

    for gap in (2, 1, 3):
        for copy in tp_copies(gap):
            copy.start()

    kv_hop(1)
    w_arrived((0, 1))
    half_copy(1, 0, 0, right_x).start()
    w_arrived((0, 2))
    half_copy(2, 32, 1, left_x).start()
    for xs in range(3):
        w_spread_z(xs)
    swaps[2].wait()

    def attend(slot, masked):
        for j in range(4):
            cols = pl.ds(j * 256, 256)
            s = jnp.dot(kbuf[slot], qt[:, cols], preferred_element_type=F32) * SCALE
            if masked:
                key = lax.broadcasted_iota(jnp.int32, (256, 256), 0)
                row = lax.broadcasted_iota(jnp.int32, (256, 256), 1) % 128 + (j // 2) * 128
                s = jnp.where(key <= row, s, -1e30)
            m_old = m_ref[:, cols]
            m_new = jnp.maximum(m_old, jnp.max(s, axis=0, keepdims=True))
            p = jnp.exp2(s - m_new)
            alpha = jnp.exp2(m_old - m_new)
            m_ref[:, cols] = m_new
            l_ref[:, cols] = l_ref[:, cols] * alpha + jnp.sum(p, axis=0, keepdims=True)
            acc[:, cols] = acc[:, cols] * alpha + jnp.dot(
                vtbuf[slot], p.astype(BF), preferred_element_type=F32
            )

    def z_of(zs):
        return (z + 8 + (1 - 2 * (zs % 2)) * ((zs + 1) // 2)) % 8

    def attend_earlier(xs, zs):
        source = ((x + X_OFFSET[xs]) % 4) * 8 + z_of(zs)

        @pl.when(source < chip)
        def _():
            attend((xs, zs), False)

    attend((0, 0), True)

    loads["ld"].wait()
    rate = -LOG2E * jnp.exp(ld_ref[...])
    for j in range(16):
        decay[pl.ds(j, 16, stride=16), :] = rate[:, j * 128:(j + 1) * 128]
    loads["du"].wait()
    loads["db"].wait()
    for gap in (1, 3, 2):
        for copy in tp_copies(gap):
            copy.wait()
    gsum[...] = gpart[...] + gland[0] + gland[1] + gland[2]
    to_scalars = pltpu.make_async_copy(gsum, gates, load_sem.at[0])
    to_scalars.start()
    low = (
        dpart[...].astype(F32) + dland[0].astype(F32) + dland[1].astype(F32) + dland[2].astype(F32)
    ).astype(BF)
    for c in range(8):
        cols = slice(c * 256, (c + 1) * 256)
        raw = jnp.dot(low, du_ref[:, cols], preferred_element_type=F32) + db_ref[:, cols]
        size = jnp.maximum(raw, 0.0) + jnp.log1p(jnp.exp(-jnp.abs(raw)))
        drive = size * act[:, cols].astype(F32)
        for half in range(2):
            j = c * 2 + half
            steps[pl.ds(j, 128, stride=16), :] = size[:, half * 128:(half + 1) * 128]
            inject[pl.ds(j, 128, stride=16), :] = drive[:, half * 128:(half + 1) * 128]
    kv_hop(2)
    half_copy(1, 0, 0, right_x).wait_recv()
    half_copy(2, 32, 1, left_x).wait_recv()
    w_spread_z(3)
    to_scalars.wait()

    def rows_of(t):
        return pl.ds(pl.multiple_of(t * 16, 16), 16)

    def first_pass(half):
        base = half * 8
        rates = [decay[(base + n) * 16:(base + n + 1) * 16, :] for n in range(8)]

        def advance(t, carried):
            size = steps[rows_of(t), :]
            drive = inject[rows_of(t), :]
            out = [
                jnp.exp2(rates[n] * size) * carried[n] + gates[base + n, t] * drive
                for n in range(8)
            ]
            return tuple(out) + (carried[8] + size,)

        zero = jnp.zeros((16, 128), F32)
        last = lax.fori_loop(0, 128, advance, (zero,) * 9, unroll=2)
        for n in range(8):
            ends[base + n] = last[n]
        if half == 0:
            total[...] = last[8]

    first_pass(0)
    kv_hop(3)
    first_pass(1)

    def col_copies(gap):
        peer = col_peer(gap)
        return (
            remote(ends.at[(k + gap) % 16], ends_in.at[gap], col_send.at[0, gap], col_recv.at[0, gap], peer),
            remote(total, total_in.at[gap], col_send.at[1, gap], col_recv.at[1, gap], peer),
        )

    def col_start(gap, _):
        for copy in col_copies(gap):
            copy.start()
        return 0

    def col_wait(gap, _):
        for copy in col_copies(gap):
            copy.wait()
        return 0

    lax.fori_loop(1, 16, col_start, 0)
    ends_in[0] = ends[k]
    total_in[0] = total[...]
    kv_hop(4)

    def x_copy(gap):
        return remote(column, column_in.at[gap - 1], x_send.at[gap], x_recv.at[gap], x_peer(gap))

    def column_stage():
        lax.fori_loop(1, 16, col_wait, 0)
        my_rate = decay[rows_of(k), :]

        def chain(j, carried):
            state, sizes = carried
            before[j] = state
            shift[j] = sizes
            slot = (k + 16 - j) % 16
            size = total_in[slot]
            return (jnp.exp2(my_rate * size) * state + ends_in[slot], sizes + size)

        zero = jnp.zeros((16, 128), F32)
        state, sizes = lax.fori_loop(0, 16, chain, (zero, zero))
        column[0] = state
        column[1] = sizes
        for gap in (2, 1, 3):
            x_copy(gap).start()

    def back_copy(gap):
        return remote(
            entry_out.at[(k + gap) % 16], entry.at[k], back_send.at[gap], back_recv.at[gap], col_peer(gap)
        )

    def back_arrival(gap):
        return remote(
            entry_out.at[(k + gap) % 16], entry.at[(k + 16 - gap) % 16],
            back_send.at[gap], back_recv.at[gap], col_peer(gap),
        )

    def back_start(gap, _):
        back_copy(gap).start()
        return 0

    def back_wait(gap, _):
        back_copy(gap).wait_send()
        back_arrival(gap).wait_recv()
        return 0

    def entry_stage():
        for gap in (1, 3, 2):
            x_copy(gap).wait()
        my_rate = decay[rows_of(k), :]
        incoming = jnp.zeros((16, 128), F32)
        for xs in range(3):
            slot = jnp.minimum((x + 3 - xs) % 4, 2)
            ahead = jnp.exp2(my_rate * column_in[slot, 1]) * incoming + column_in[slot, 0]
            incoming = jnp.where(xs < x, ahead, incoming)

        def finish(j, _):
            entry_out[j] = before[j] + jnp.exp2(my_rate * shift[j]) * incoming
            return 0

        lax.fori_loop(0, 16, finish, 0)
        lax.fori_loop(1, 16, back_start, 0)
        entry[k] = entry_out[k]

    def w_event(e):
        h = 1 + e // 4
        xs = e % 4
        w_arrived((2 * h - 1, xs))

        @pl.when((h < 3) | (xs < 2))
        def _():
            w_copy((2 * h - 1, xs), (2 * h + 1, xs), right_z).start()

        w_arrived((2 * h, xs))

        @pl.when(h < 3)
        def _():
            w_copy((2 * h, xs), (2 * h + 2, xs), left_z).start()

        @pl.when((h == 3) & (xs >= 2))
        def _():
            w_copy((2 * h, xs), (7, xs), left_z).start()

    def sweep(i, _):
        for kind in (0, 1):
            kv_arrived(kind, (1, i))

            @pl.when(i < 4)
            def _():
                kv_copy(kind, (1, i), (3, i), right_x).start()

            kv_arrived(kind, (2, i))

            @pl.when(i >= 4)
            def _():
                kv_copy(kind, (2, i), (3, i), left_x).start()

        w_event(i)

        @pl.when(i > 0)
        def _():
            attend_earlier(0, i)

        attend_earlier(1, i)
        attend_earlier(2, i)

        @pl.when(i > 0)
        def _():
            for kind in (0, 1):
                kv_arrived(kind, (3, i - 1))
            attend_earlier(3, i - 1)

        @pl.when(i == 2)
        def _():
            column_stage()

        @pl.when(i == 4)
        def _():
            entry_stage()

        return 0

    lax.fori_loop(0, 8, sweep, 0)
    for kind in (0, 1):
        kv_arrived(kind, (3, 7))
    attend_earlier(3, 7)

    inverse = 1.0 / l_ref[...]
    heads = []
    for h in range(4):
        pieces = []
        for r in range(2):
            cols = slice(r * 512 + h * 128, r * 512 + (h + 1) * 128)
            pieces.append((acc[:, cols] * inverse[:, cols]).astype(BF))
        heads.append(jnp.concatenate(pieces, axis=1))
    att[own_cols, :] = jnp.concatenate(heads, axis=0)
    att_swap = pair_copy(att.at[own_cols, :], att.at[own_cols, :], 3)
    att_swap.start()
    lax.fori_loop(1, 16, back_wait, 0)

    def second_pass(half):
        base = half * 8
        rates = [decay[(base + n) * 16:(base + n + 1) * 16, :] for n in range(8)]

        def advance(t, carried):
            size = steps[rows_of(t), :]
            drive = inject[rows_of(t), :]
            out = []
            mixed = scanned[rows_of(t), :] if half else None
            for n in range(8):
                state = jnp.exp2(rates[n] * size) * carried[n] + gates[base + n, t] * drive
                term = gates[NS + base + n, t] * state
                mixed = term if mixed is None else mixed + term
                out.append(state)
            scanned[rows_of(t), :] = mixed
            return tuple(out)

        lax.fori_loop(0, 128, advance, tuple(entry[base + n] for n in range(8)), unroll=2)

    def slot_of(gap):
        d = (y + gap + 4 - x) % 4
        return 2 * d - d // 2 - 4 * (d // 3)

    def y_copy(gap, r, g):
        first, count = GROUPS[g]
        rows = pl.ds(first, count)
        return remote(
            stage.at[slot_of(gap), r, rows], landed.at[gap, core, rows],
            y_send.at[gap, r, g], y_recv.at[gap, core, g], at(chip * 2 + r, (y + gap) % 4),
        )

    def y_arrival(gap, c, g):
        first, count = GROUPS[g]
        rows = pl.ds(first, count)
        return remote(
            stage.at[0, 0, rows], landed.at[gap, c, rows],
            y_send.at[gap, c, g], y_recv.at[gap, c, g], partner,
        )

    def project(g):
        first, count = GROUPS[g]
        for zs in range(first, first + count):
            part = jnp.dot(
                wbuf[zs].reshape(256, 1024), att[...], preferred_element_type=F32
            ).astype(BF)
            for xs in range(4):
                for r in range(2):
                    stage[xs, r, zs] = part[xs * 64:(xs + 1) * 64, r * 128:(r + 1) * 128]
        for gap in (2, 1, 3):
            for r in range(2):
                y_copy(gap, r, g).start()
        y_copy_partner(g).start()
        for zs in range(first, first + count):
            landed[0, core, zs] = stage[slot_of(0), core, zs]

    def y_copy_partner(g):
        first, count = GROUPS[g]
        rows = pl.ds(first, count)
        return remote(
            stage.at[slot_of(0), other, rows], landed.at[0, core, rows],
            y_send.at[0, 0, g], y_recv.at[0, core, g], partner,
        )

    second_pass(0)
    att_swap.wait()
    project(0)
    project(1)

    def late_event(e, _):
        w_event(e)
        return 0

    lax.fori_loop(8, 12, late_event, 0)
    project(2)
    second_pass(1)
    project(3)
    loads["z"].wait()
    loads["sg"].wait()
    for j in range(16):
        cols = slice(j * 128, (j + 1) * 128)
        gate = z_ref[:, cols].astype(F32)
        mixed = scanned[pl.ds(j, 128, stride=16), :] + sg_ref[:, cols] * act[:, cols].astype(F32)
        mix_ref[:, cols] = (mixed * (gate / (1.0 + jnp.exp(-gate)))).astype(BF)
    for xs in range(4):
        w_arrived((7, xs))
    project(4)

    loads["res"].wait()
    for g in range(5):
        y_arrival(0, other, g).wait_recv()
        for gap in (1, 3, 2):
            for c in range(2):
                y_arrival(gap, c, g).wait_recv()
        first, count = GROUPS[g]
        for zs in range(first, first + count):
            for c in range(2):
                part = landed[0, c, zs].astype(F32)
                for gap in range(1, 4):
                    part = part + landed[gap, c, zs].astype(F32)
                rows = pl.ds(pl.multiple_of(z_of(zs) * 128 + c * 64, 64), 64)
                out_t[rows, :] = part
    for zo in range(8):
        cols = slice(zo * 128, (zo + 1) * 128)
        out_ref[:, cols] = (res_ref[:, cols].astype(F32) + out_t[cols, :].T).astype(BF)

    for g in range(5):
        y_copy_partner(g).wait_send()
        for gap in (1, 2, 3):
            for r in range(2):
                y_copy(gap, r, g).wait_send()
    for i in range(2):
        half_copy(i + 1, 32 * i, i, right_x).wait_send()
    w_copy((0, 0), (0, 1), right_x).wait_send()
    w_copy((0, 0), (0, 2), left_x).wait_send()

    def drain(zs, _):
        for kind in (0, 1):
            @pl.when((zs > 0) & (zs < 7))
            def _():
                kv_copy(kind, (0, zs), (0, zs), right_z).wait_send()

            for xs in range(1, 4):
                kv_copy(kind, (xs, zs), (xs, zs), right_z).wait_send()

        @pl.when(zs > 0)
        def _():
            for xs in range(4):
                w_copy((zs, xs), (zs, xs), right_z).wait_send()

        return 0

    lax.fori_loop(0, 8, drain, 0)
    for kind in (0, 1):
        kv_copy(kind, (0, 7), (0, 7), right_z).wait_send()


def block(
    x_stream, z_stream, conv_kernel, conv_bias, delta_down, state_proj, delta_up, delta_bias,
    log_decay, skip_gain, queries, key_heads, values, out_proj, residual,
):
    dma = pltpu.SemaphoreType.DMA
    operands = (
        x_stream, z_stream, conv_kernel, conv_bias[None, :], delta_down, state_proj, delta_up,
        delta_bias[None, :], log_decay, skip_gain[None, :], queries, key_heads, values, out_proj.T, residual,
    )
    copies = [pltpu.VMEM(a.shape, a.dtype) for i, a in enumerate(operands) if i != 13]
    states = pltpu.VMEM((16, 16, 128), F32)
    by_token = pltpu.VMEM((2048, 128), F32)
    return pl.pallas_call(
        block_kernel,
        out_shape=(
            jax.ShapeDtypeStruct(x_stream.shape, BF), jax.ShapeDtypeStruct(residual.shape, BF)
        ),
        in_specs=[pl.BlockSpec(memory_space=pl.ANY)] * 15,
        out_specs=(pl.BlockSpec(memory_space=pltpu.VMEM),) * 2,
        scratch_shapes=copies + [
            pltpu.VMEM((2, 128, 512), BF),
            pltpu.VMEM((256, 128), BF),
            pltpu.VMEM((128, 1024), BF),
            pltpu.VMEM((4, 8, 256, 128), BF),
            pltpu.VMEM((4, 8, 128, 256), BF),
            pltpu.VMEM((8, 4, 64, 1024), BF),
            pltpu.VMEM((1, 1024), F32),
            pltpu.VMEM((1, 1024), F32),
            pltpu.VMEM((128, 1024), F32),
            pltpu.VMEM((1024, 256), BF),
            pltpu.VMEM((4, 2, 8, 64, 128), BF),
            pltpu.VMEM((4, 2, 8, 64, 128), BF),
            pltpu.VMEM((1024, 128), F32),
            pltpu.VMEM((16, 2048), BF),
            pltpu.VMEM((136, 2048), F32),
            pltpu.VMEM((128, 2048), BF),
            pltpu.VMEM((128, 256), BF),
            pltpu.VMEM((32, 128), F32),
            pltpu.VMEM((3, 128, 256), BF),
            pltpu.VMEM((3, 32, 128), F32),
            pltpu.VMEM((32, 128), F32),
            pltpu.SMEM((32, 128), F32),
            by_token, by_token, by_token,
            pltpu.VMEM((256, 128), F32),
            states,
            pltpu.VMEM((16, 128), F32),
            states, states, states, states,
            pltpu.VMEM((2, 16, 128), F32),
            pltpu.VMEM((3, 2, 16, 128), F32),
            states, states,
            dma((15,)), dma((4,)), dma((4,)), dma((2, 4, 8)), dma((2, 4, 8)), dma((8, 4)), dma((8, 4)),
            dma((2,)), dma((2,)), dma((4, 2, 5)), dma((4, 2, 5)), dma((1,)), dma((1,)),
            dma((2, 4)), dma((2, 4)), dma((2, 16)), dma((2, 16)), dma((4,)), dma((4,)),
            dma((16,)), dma((16,)),
        ],
        compiler_params=pltpu.CompilerParams(
            collective_id=0, has_side_effects=True, vmem_limit_bytes=56 * 1024 * 1024
        ),
    )(*operands)


def solution(mesh):
    both = P("ctx", "tp")
    placed = (
        both, both, P(None, "tp"), P("tp"), P("tp", None), P(None, "tp"), P(None, "tp"), P("tp"),
        P(None, "tp"), P("tp"), both, both, both, P("tp", "ctx"), both,
    )
    return jax.shard_map(
        block, mesh=mesh, in_specs=placed, out_specs=(both, both), check_vma=False
    )
```

```python
import math

import jax
import jax.numpy as jnp
from jax import lax
from jax.experimental import pallas as pl
from jax.experimental.pallas import tpu as pltpu
from jax.sharding import PartitionSpec as P

HD = 128
NS = 16
BF = jnp.bfloat16
F32 = jnp.float32
MESH = pl.DeviceIdType.MESH
LOG2E = math.log2(math.e)
SCALE = LOG2E / math.sqrt(HD)
X_OFFSET = (0, 3, 1, 2)
WIDE = 512
LOW = 16
GROUPS = ((0, 1), (1, 2), (3, 2), (5, 2), (7, 1))


def at(ctx, tp):
    return {"ctx": ctx, "tp": tp}


def remote(src, dst, send, recv, peer):
    return pltpu.make_async_remote_copy(
        src_ref=src, dst_ref=dst, send_sem=send, recv_sem=recv, device_id=peer, device_id_type=MESH
    )


def block_kernel(
    x_hbm, z_hbm, ck_hbm, cb_hbm, dd_hbm, sp_hbm, du_hbm, db_hbm, ld_hbm, sg_hbm,
    q_hbm, k_hbm, v_hbm, wt_hbm, res_hbm, mix_ref, out_ref,
    x_ref, z_ref, ck_ref, cb_ref, dd_ref, sp_ref, du_ref, db_ref, ld_ref, sg_ref,
    q_ref, k_ref, v_ref, res_ref,
    qts, vts, qt, kbuf, vtbuf, wlow, wbuf, m_ref, l_ref, acc, att, stage, landed, stage_low, landed_low, out_t,
    rim, padded, act, dpart, gpart, dland, gland, gsum, gates, steps, inject, scanned, decay,
    ends, ends_in, before, shift, column, column_in, entry_out, entry,
    load_sem, pair_send, pair_recv, kv_send, kv_recv, w_send, w_recv, half_send, half_recv,
    y_send, y_recv, rim_send, rim_recv, tp_send, tp_recv, col_send, col_recv, x_send, x_recv,
    back_send, back_recv,
):
    me = lax.axis_index("ctx")
    y = lax.axis_index("tp")
    core = me % 2
    other = 1 - core
    chip = me // 2
    z = chip % 8
    x = me // 16
    k = me % 16
    partner = at(me + 1 - 2 * core, y)
    after = at((me + 1) % 64, y)
    earlier = at((me + 63) % 64, y)
    right_z = at(x * 16 + ((z + 1) % 8) * 2 + core, y)
    left_z = at(x * 16 + ((z + 7) % 8) * 2 + core, y)
    right_x = at(((x + 1) % 4) * 16 + k, y)
    left_x = at(((x + 3) % 4) * 16 + k, y)

    def col_peer(gap):
        return at(x * 16 + (k + gap) % 16, y)

    def x_peer(gap):
        return at(((x + gap) % 4) * 16 + k, y)

    barrier = pltpu.get_barrier_semaphore()

    def greet(peer):
        pl.semaphore_signal(barrier, inc=1, device_id=peer, device_id_type=MESH)

    greet(after)
    greet(earlier)
    for gap in (1, 2, 3):
        greet(x_peer(gap))
        for r in range(2):
            greet(at(chip * 2 + r, (y + gap) % 4))
    for gap in range(1, 16):
        greet(col_peer(gap))

    loads = {}
    pairs = (
        ("v", v_hbm, v_ref), ("k", k_hbm, k_ref), ("w", wt_hbm.at[pl.ds(LOW, 64 - LOW)], wbuf.at[0, 0]), ("wl", wt_hbm.at[pl.ds(0, LOW)], wlow.at[0, 0]), ("q", q_hbm, q_ref),
        ("x", x_hbm, x_ref), ("ck", ck_hbm, ck_ref), ("cb", cb_hbm, cb_ref), ("dd", dd_hbm, dd_ref),
        ("sp", sp_hbm, sp_ref), ("ld", ld_hbm, ld_ref), ("du", du_hbm, du_ref), ("db", db_hbm, db_ref),
        ("z", z_hbm, z_ref), ("sg", sg_hbm, sg_ref), ("res", res_hbm, res_ref),
    )
    for i, (name, src, dst) in enumerate(pairs):
        loads[name] = pltpu.make_async_copy(src, dst, load_sem.at[i])
        loads[name].start()

    loads["v"].wait()
    vts[...] = v_ref[...].astype(F32).T.astype(BF)
    loads["q"].wait()
    for g in range(2):
        for h in range(4):
            head = q_ref[:, (g * 4 + h) * HD:(g * 4 + h + 1) * HD]
            qts[g, :, h * HD:(h + 1) * HD] = head.astype(F32).T.astype(BF)
    m_ref[...] = jnp.full_like(m_ref, -1e30)
    l_ref[...] = jnp.zeros_like(l_ref)
    acc[...] = jnp.zeros_like(acc)

    def convolve(count):
        for c in range(8):
            cols = slice(c * 256, (c + 1) * 256)
            conv = cb_ref[:, cols]
            for tap in range(4):
                conv = conv + ck_ref[tap:tap + 1, cols] * padded[5 + tap:5 + tap + count, cols]
            act[:count, cols] = (conv / (1.0 + jnp.exp(-conv))).astype(BF)

    loads["x"].wait()
    loads["ck"].wait()
    loads["cb"].wait()
    padded[:8, :] = jnp.zeros((8, 2048), F32)
    padded[8:, :] = x_ref[...].astype(F32)
    convolve(128)
    loads["ld"].wait()
    rate = -LOG2E * jnp.exp(ld_ref[...])
    for j in range(16):
        decay[pl.ds(j, 16, stride=16), :] = rate[:, j * 128:(j + 1) * 128]
    loads["k"].wait()
    loads["w"].wait()
    loads["wl"].wait()
    pl.semaphore_wait(barrier, 26)

    own_rows = pl.ds(pl.multiple_of(core * 128, 128), 128)
    other_rows = pl.ds(pl.multiple_of(other * 128, 128), 128)
    own_cols = pl.ds(pl.multiple_of(core * 512, 512), 512)

    def pair_copy(src, dst, i):
        return remote(src, dst, pair_send.at[i], pair_recv.at[i], partner)

    swaps = (
        pair_copy(k_ref.at[:, other_rows], kbuf.at[0, 0, own_rows, :], 0),
        pair_copy(vts.at[other_rows, :], vtbuf.at[0, 0, :, own_rows], 1),
        pair_copy(qts.at[other], qt.at[:, own_cols], 2),
    )
    for swap in swaps:
        swap.start()

    bufs = (kbuf, vtbuf, wlow)

    def kv_copy(kind, src, dst, peer):
        return remote(
            bufs[kind].at[src], bufs[kind].at[dst], kv_send.at[(kind, *dst)], kv_recv.at[(kind, *dst)], peer
        )

    def kv_arrived(kind, slot):
        kv_copy(kind, slot, slot, right_z).wait_recv()

    def spread_x(kind, zs):
        kv_copy(kind, (0, zs), (1, zs), right_x).start()
        kv_copy(kind, (0, zs), (2, zs), left_x).start()

    def w_copy(src, dst, peer):
        return remote(wbuf.at[src], wbuf.at[dst], w_send.at[dst], w_recv.at[dst], peer)

    def w_arrived(slot):
        w_copy(slot, slot, right_z).wait_recv()

    def half_copy(source, rows, i, peer):
        half = pl.ds(rows, 32 - rows // 2)
        return remote(
            wbuf.at[0, source, half, :], wbuf.at[0, 3, half, :], half_send.at[i], half_recv.at[i], peer
        )

    def w_spread_z(xs):
        w_copy((0, xs), (1, xs), right_z).start()
        w_copy((0, xs), (2, xs), left_z).start()

    w_copy((0, 0), (0, 1), right_x).start()
    w_copy((0, 0), (0, 2), left_x).start()
    kbuf[0, 0, own_rows, :] = k_ref[:, own_rows]
    vtbuf[0, 0, :, own_rows] = vts[own_rows, :]
    rim_copy = remote(x_ref.at[pl.ds(112, 16), :], rim, rim_send.at[0], rim_recv.at[0], after)
    rim_copy.start()
    qt[:, own_cols] = qts[core]
    for kind in (0, 1):
        swaps[kind].wait()
        kv_copy(kind, (0, 0), (0, 1), right_z).start()
        kv_copy(kind, (0, 0), (0, 2), left_z).start()
        spread_x(kind, 0)
    w_spread_z(0)

    def low_hop(h):
        if h == 0:
            kv_copy(2, (0, 0), (0, 1), right_z).start()
            kv_copy(2, (0, 0), (0, 2), left_z).start()
        elif h < 4:
            kv_arrived(2, (0, 2 * h - 1))
            kv_copy(2, (0, 2 * h - 1), (0, 2 * h + 1), right_z).start()
            kv_arrived(2, (0, 2 * h))
            if h < 3:
                kv_copy(2, (0, 2 * h), (0, 2 * h + 2), left_z).start()
        else:
            kv_arrived(2, (0, 7))

    def kv_hop(h):
        for kind in (0, 1):
            if h < 4:
                kv_arrived(kind, (0, 2 * h - 1))
                if h < 3:
                    kv_copy(kind, (0, 2 * h - 1), (0, 2 * h + 1), right_z).start()
                elif kind == 0:
                    kv_copy(kind, (0, 5), (0, 7), right_z).start()
                spread_x(kind, 2 * h - 1)
                kv_arrived(kind, (0, 2 * h))
                if h < 3:
                    kv_copy(kind, (0, 2 * h), (0, 2 * h + 2), left_z).start()
                elif kind == 1:
                    kv_copy(kind, (0, 6), (0, 7), left_z).start()
                spread_x(kind, 2 * h)
            else:
                kv_arrived(kind, (0, 7))
                spread_x(kind, 7)

    def attend(slots, biases):
        def scores(j):
            cols = slice(j * WIDE, (j + 1) * WIDE)
            return [jnp.dot(kbuf[slot], qt[:, cols], preferred_element_type=F32) for slot in slots]

        following = scores(0)
        for j in range(1024 // WIDE):
            cols = slice(j * WIDE, (j + 1) * WIDE)
            now = following
            if (j + 1) * WIDE < 1024:
                following = scores(j + 1)
            if biases is None:
                key = lax.broadcasted_iota(jnp.int32, (256, WIDE), 0)
                row = lax.broadcasted_iota(jnp.int32, (256, WIDE), 1) % 128 + (j * WIDE // 512) * 128
                now = [jnp.where(key <= row, s, -1e30) for s in now]
            m_old = m_ref[:, cols]
            m_new = m_old
            for i, s in enumerate(now):
                top = jnp.max(s, axis=0, keepdims=True) * SCALE
                m_new = jnp.maximum(m_new, top if biases is None else top + biases[i])
            alpha = jnp.exp2(m_old - m_new)
            gained = l_ref[:, cols] * alpha
            mixed = acc[:, cols] * alpha
            for i, s in enumerate(now):
                p = jnp.exp2(s * SCALE - (m_new if biases is None else m_new - biases[i]))
                gained = gained + jnp.sum(p, axis=0, keepdims=True)
                mixed = mixed + jnp.dot(vtbuf[slots[i]], p.astype(BF), preferred_element_type=F32)
            m_ref[:, cols] = m_new
            l_ref[:, cols] = gained
            acc[:, cols] = mixed

    def z_of(zs):
        return (z + 8 + (1 - 2 * (zs % 2)) * ((zs + 1) // 2)) % 8

    def attend_earlier(first, second, zs):
        earlier_than = [((x + X_OFFSET[xs]) % 4) * 8 + z_of(zs) < chip for xs in (first, second)]

        @pl.when(earlier_than[0] | earlier_than[1])
        def _():
            attend(
                [(xs, zs) for xs in (first, second)],
                [jnp.where(flag, 0.0, -1e30).astype(F32) for flag in earlier_than],
            )

    swaps[2].wait()
    attend([(0, 0)], None)

    rim_copy.wait()
    padded[:8, :] = jnp.where(me > 0, rim[8:, :].astype(F32), 0.0)
    convolve(16)
    loads["dd"].wait()
    loads["sp"].wait()
    dpart[...] = jnp.dot(act[...], dd_ref[...], preferred_element_type=F32).astype(BF)
    gpart[...] = lax.dot_general(
        sp_ref[...], act[...], (((1,), (1,)), ((), ())), preferred_element_type=F32
    )

    def tp_copies(gap):
        peer = at(me, (y + gap) % 4)
        return (
            remote(dpart, dland.at[gap - 1], tp_send.at[0, gap], tp_recv.at[0, gap], peer),
            remote(gpart, gland.at[gap - 1], tp_send.at[1, gap], tp_recv.at[1, gap], peer),
        )

    for gap in (2, 1, 3):
        for copy in tp_copies(gap):
            copy.start()


    kv_hop(1)
    w_arrived((0, 1))
    half_copy(1, 0, 0, right_x).start()
    w_arrived((0, 2))
    half_copy(2, 32, 1, left_x).start()
    w_spread_z(1)
    low_hop(0)

    def step_stage():
        loads["du"].wait()
        loads["db"].wait()
        for gap in (1, 3, 2):
            for copy in tp_copies(gap):
                copy.wait()
        gsum[...] = gpart[...] + gland[0] + gland[1] + gland[2]
        to_scalars = pltpu.make_async_copy(gsum, gates, load_sem.at[0])
        to_scalars.start()
        low = (
            dpart[...].astype(F32) + dland[0].astype(F32) + dland[1].astype(F32) + dland[2].astype(F32)
        ).astype(BF)
        for c in range(8):
            cols = slice(c * 256, (c + 1) * 256)
            raw = jnp.dot(low, du_ref[:, cols], preferred_element_type=F32) + db_ref[:, cols]
            size = jnp.maximum(raw, 0.0) + jnp.log1p(jnp.exp(-jnp.abs(raw)))
            drive = size * act[:, cols].astype(F32)
            for half in range(2):
                j = c * 2 + half
                steps[pl.ds(j, 128, stride=16), :] = size[:, half * 128:(half + 1) * 128]
                inject[pl.ds(j, 128, stride=16), :] = drive[:, half * 128:(half + 1) * 128]
        to_scalars.wait()

    def rows_of(t):
        return pl.ds(pl.multiple_of(t * 16, 16), 16)

    def first_pass(half):
        base = half * 8
        rates = [decay[(base + n) * 16:(base + n + 1) * 16, :] for n in range(8)]

        def advance(t, carried):
            size = steps[rows_of(t), :]
            drive = inject[rows_of(t), :]
            out = [
                jnp.exp2(rates[n] * size) * carried[n] + gates[base + n, t] * drive
                for n in range(8)
            ]
            return tuple(out) + (carried[8] + size,)

        zero = jnp.zeros((16, 128), F32)
        last = lax.fori_loop(0, 128, advance, (zero,) * 9, unroll=2)
        for n in range(8):
            ends[base + n, 0] = last[n].astype(BF)
            ends[base + n, 1] = last[8].astype(BF)

    def col_copies(gap):
        peer = col_peer(gap)
        return (
            remote(ends.at[(k + gap) % 16], ends_in.at[gap], col_send.at[gap], col_recv.at[gap], peer),
        )

    def col_start(gap, _):
        for copy in col_copies(gap):
            copy.start()
        return 0

    def col_wait(gap, _):
        for copy in col_copies(gap):
            copy.wait()
        return 0

    def ends_stage():
        lax.fori_loop(1, 16, col_start, 0)
        ends_in[0] = ends[k]

    def x_copy(gap):
        return remote(column, column_in.at[gap - 1], x_send.at[gap], x_recv.at[gap], x_peer(gap))

    def column_stage():
        lax.fori_loop(1, 16, col_wait, 0)
        my_rate = decay[rows_of(k), :]

        def chain(j, carried):
            state, sizes = carried
            before[j] = state
            shift[j] = sizes
            slot = (k + 16 - j) % 16
            size = ends_in[slot, 1].astype(F32)
            return (jnp.exp2(my_rate * size) * state + ends_in[slot, 0].astype(F32), sizes + size)

        zero = jnp.zeros((16, 128), F32)
        state, sizes = lax.fori_loop(0, 16, chain, (zero, zero))
        column[0] = state
        column[1] = sizes
        for gap in (2, 1, 3):
            x_copy(gap).start()

    def back_copy(gap):
        return remote(
            entry_out.at[(k + gap) % 16], entry.at[k], back_send.at[gap], back_recv.at[gap], col_peer(gap)
        )

    def back_arrival(gap):
        return remote(
            entry_out.at[(k + gap) % 16], entry.at[(k + 16 - gap) % 16],
            back_send.at[gap], back_recv.at[gap], col_peer(gap),
        )

    def back_start(gap, _):
        back_copy(gap).start()
        return 0

    def back_wait(gap, _):
        back_copy(gap).wait_send()
        back_arrival(gap).wait_recv()
        return 0

    def entry_stage():
        for gap in (1, 3, 2):
            x_copy(gap).wait()
        my_rate = decay[rows_of(k), :]
        incoming = jnp.zeros((16, 128), F32)
        for xs in range(3):
            slot = jnp.minimum((x + 3 - xs) % 4, 2)
            ahead = jnp.exp2(my_rate * column_in[slot, 1]) * incoming + column_in[slot, 0]
            incoming = jnp.where(xs < x, ahead, incoming)

        def finish(j, _):
            entry_out[j] = (before[j] + jnp.exp2(my_rate * shift[j]) * incoming).astype(BF)
            return 0

        lax.fori_loop(0, 16, finish, 0)
        lax.fori_loop(1, 16, back_start, 0)
        entry[k] = entry_out[k]

    def w_event(e):
        h = 1 + e // 4
        xs = e % 4
        w_arrived((2 * h - 1, xs))

        @pl.when((h < 3) | (xs < 2))
        def _():
            w_copy((2 * h - 1, xs), (2 * h + 1, xs), right_z).start()

        w_arrived((2 * h, xs))

        @pl.when(h < 3)
        def _():
            w_copy((2 * h, xs), (2 * h + 2, xs), left_z).start()

        @pl.when((h == 3) & (xs >= 2))
        def _():
            w_copy((2 * h, xs), (7, xs), left_z).start()

    def sweep(i, _):
        @pl.when(i == 1)
        def _():
            kv_hop(2)
            low_hop(1)
            w_spread_z(2)

        @pl.when(i == 2)
        def _():
            kv_hop(3)
            low_hop(2)
            half_copy(1, 0, 0, right_x).wait_recv()
            half_copy(2, 32, 1, left_x).wait_recv()
            w_spread_z(3)

        @pl.when(i == 3)
        def _():
            kv_hop(4)
            low_hop(3)

        for kind, near, peer in ((0, 1, right_x), (1, 2, left_x)):
            kv_arrived(kind, (1, i))
            kv_arrived(kind, (2, i))
            kv_copy(kind, (near, i), (3, i), peer).start()

        @pl.when(i >= 2)
        def _():
            w_event(i - 2 + i // 7)

        attend_earlier(1, 2, i)

        @pl.when(i == 6)
        def _():
            w_event(5)

        @pl.when(i == 0)
        def _():
            step_stage()

        @pl.when(i == 1)
        def _():
            first_pass(0)

        @pl.when(i == 2)
        def _():
            first_pass(1)
            ends_stage()

        @pl.when(i > 0)
        def _():
            for kind in (0, 1):
                kv_arrived(kind, (3, i - 1))
            attend_earlier(0, 3, i - 1)

        @pl.when(i == 4)
        def _():
            column_stage()

        @pl.when(i == 6)
        def _():
            entry_stage()

        return 0

    lax.fori_loop(0, 8, sweep, 0)
    for kind in (0, 1):
        kv_arrived(kind, (3, 7))
    attend_earlier(0, 3, 7)

    low_hop(4)

    def low_spread(zs, _):
        spread_x(2, zs)
        return 0

    lax.fori_loop(0, 8, low_spread, 0)
    inverse = 1.0 / l_ref[...]
    heads = []
    for h in range(4):
        pieces = []
        for r in range(2):
            cols = slice(r * 512 + h * 128, r * 512 + (h + 1) * 128)
            pieces.append((acc[:, cols] * inverse[:, cols]).astype(BF))
        heads.append(jnp.concatenate(pieces, axis=1))
    att[own_cols, :] = jnp.concatenate(heads, axis=0)
    att_swap = pair_copy(att.at[own_cols, :], att.at[own_cols, :], 3)
    att_swap.start()
    lax.fori_loop(1, 16, back_wait, 0)

    def second_pass(half):
        base = half * 8
        rates = [decay[(base + n) * 16:(base + n + 1) * 16, :] for n in range(8)]

        def advance(t, carried):
            size = steps[rows_of(t), :]
            drive = inject[rows_of(t), :]
            out = []
            mixed = scanned[rows_of(t), :] if half else None
            for n in range(8):
                state = jnp.exp2(rates[n] * size) * carried[n] + gates[base + n, t] * drive
                term = gates[NS + base + n, t] * state
                mixed = term if mixed is None else mixed + term
                out.append(state)
            scanned[rows_of(t), :] = mixed
            return tuple(out)

        lax.fori_loop(0, 128, advance, tuple(entry[base + n].astype(F32) for n in range(8)), unroll=2)

    def slot_of(gap):
        d = (y + gap + 4 - x) % 4
        return 2 * d - d // 2 - 4 * (d // 3)

    def y_copy(gap, r, g):
        first, count = GROUPS[g]
        rows = pl.ds(first, count)
        return remote(
            stage.at[slot_of(gap), r, rows], landed.at[gap, core, rows],
            y_send.at[gap, r, g], y_recv.at[gap, core, g], at(chip * 2 + r, (y + gap) % 4),
        )

    def y_arrival(gap, c, g):
        first, count = GROUPS[g]
        rows = pl.ds(first, count)
        return remote(
            stage.at[0, 0, rows], landed.at[gap, c, rows],
            y_send.at[gap, c, g], y_recv.at[gap, c, g], partner,
        )

    def project(g):
        first, count = GROUPS[g]
        for zs in range(first, first + count):
            part = jnp.dot(
                wbuf[zs].reshape(4 * (64 - LOW), 1024), att[...], preferred_element_type=F32
            ).astype(BF)
            for xs in range(4):
                for r in range(2):
                    stage[xs, r, zs] = part[xs * (64 - LOW):(xs + 1) * (64 - LOW), r * 128:(r + 1) * 128]
        for gap in (2, 1, 3):
            for r in range(2):
                y_copy(gap, r, g).start()
        y_copy_partner(g).start()
        for zs in range(first, first + count):
            landed[0, core, zs] = stage[slot_of(0), core, zs]

    def y_copy_partner(g):
        first, count = GROUPS[g]
        rows = pl.ds(first, count)
        return remote(
            stage.at[slot_of(0), other, rows], landed.at[0, core, rows],
            y_send.at[0, 0, g], y_recv.at[0, core, g], partner,
        )

    def low_cross(i, _):
        for zs, near, peer in ((2 * i, 1, right_x), (2 * i + 1, 2, left_x)):
            kv_arrived(2, (1, zs))
            kv_arrived(2, (2, zs))
            kv_copy(2, (near, zs), (3, zs), peer).start()
        return 0

    def y_low(gap, r):
        return remote(
            stage_low.at[slot_of(gap), r], landed_low.at[gap, core],
            y_send.at[gap, r, 5], y_recv.at[gap, core, 5], at(chip * 2 + r, (y + gap) % 4),
        )

    def y_low_partner():
        return remote(
            stage_low.at[slot_of(0), other], landed_low.at[0, core],
            y_send.at[0, 0, 5], y_recv.at[0, core, 5], partner,
        )

    def y_low_arrival(gap, c):
        return remote(
            stage_low.at[0, 0], landed_low.at[gap, c], y_send.at[gap, c, 5], y_recv.at[gap, c, 5], partner
        )

    def project_low():
        for zs in range(8):
            kv_arrived(2, (3, zs))
        for xs in range(4):
            part = jnp.dot(
                wlow[xs].reshape(8 * LOW, 1024), att[...], preferred_element_type=F32
            ).astype(BF)
            for r in range(2):
                stage_low[xs, r] = part[:, r * 128:(r + 1) * 128].reshape(8, LOW, 128)
        for gap in (2, 1, 3):
            for r in range(2):
                y_low(gap, r).start()
        y_low_partner().start()
        landed_low[0, core] = stage_low[slot_of(0), core]

    w_event(7)
    att_swap.wait()
    project(0)
    project(1)
    project(2)
    w_event(8)
    w_event(9)
    lax.fori_loop(0, 4, low_cross, 0)
    second_pass(0)
    w_event(10)
    w_event(11)
    second_pass(1)
    project(3)
    loads["z"].wait()
    loads["sg"].wait()
    for j in range(16):
        cols = slice(j * 128, (j + 1) * 128)
        gate = z_ref[:, cols].astype(F32)
        mixed = scanned[pl.ds(j, 128, stride=16), :] + sg_ref[:, cols] * act[:, cols].astype(F32)
        mix_ref[:, cols] = (mixed * (gate / (1.0 + jnp.exp(-gate)))).astype(BF)
    project_low()
    for xs in range(4):
        w_arrived((7, xs))
    project(4)

    loads["res"].wait()
    for g in range(5):
        y_arrival(0, other, g).wait_recv()
        for gap in (1, 3, 2):
            for c in range(2):
                y_arrival(gap, c, g).wait_recv()
        first, count = GROUPS[g]
        for zs in range(first, first + count):
            for c in range(2):
                part = landed[0, c, zs].astype(F32)
                for gap in range(1, 4):
                    part = part + landed[gap, c, zs].astype(F32)
                rows = pl.ds(pl.multiple_of(z_of(zs) * 128 + c * 64 + LOW, LOW), 64 - LOW)
                out_t[rows, :] = part
    y_low_arrival(0, other).wait_recv()
    for gap in (1, 3, 2):
        for c in range(2):
            y_low_arrival(gap, c).wait_recv()
    for zs in range(8):
        for c in range(2):
            part = landed_low[0, c, zs].astype(F32)
            for gap in range(1, 4):
                part = part + landed_low[gap, c, zs].astype(F32)
            rows = pl.ds(pl.multiple_of(z_of(zs) * 128 + c * 64, 64), LOW)
            out_t[rows, :] = part
    for zo in range(8):
        cols = slice(zo * 128, (zo + 1) * 128)
        out_ref[:, cols] = (res_ref[:, cols].astype(F32) + out_t[cols, :].T).astype(BF)

    for g in range(5):
        y_copy_partner(g).wait_send()
        for gap in (1, 2, 3):
            for r in range(2):
                y_copy(gap, r, g).wait_send()
    y_low_partner().wait_send()
    for gap in (1, 2, 3):
        for r in range(2):
            y_low(gap, r).wait_send()
    for i in range(2):
        half_copy(i + 1, 32 * i, i, right_x).wait_send()
    w_copy((0, 0), (0, 1), right_x).wait_send()
    w_copy((0, 0), (0, 2), left_x).wait_send()

    def drain(zs, _):
        for kind in (0, 1, 2):
            @pl.when((zs > 0) & (zs < 7))
            def _():
                kv_copy(kind, (0, zs), (0, zs), right_z).wait_send()

            for xs in range(1, 4):
                kv_copy(kind, (xs, zs), (xs, zs), right_z).wait_send()

        @pl.when(zs > 0)
        def _():
            for xs in range(4):
                w_copy((zs, xs), (zs, xs), right_z).wait_send()

        return 0

    lax.fori_loop(0, 8, drain, 0)
    for kind in (0, 1, 2):
        kv_copy(kind, (0, 7), (0, 7), right_z).wait_send()


def block(
    x_stream, z_stream, conv_kernel, conv_bias, delta_down, state_proj, delta_up, delta_bias,
    log_decay, skip_gain, queries, key_heads, values, out_proj, residual,
):
    dma = pltpu.SemaphoreType.DMA
    operands = (
        x_stream, z_stream, conv_kernel, conv_bias[None, :], delta_down, state_proj, delta_up,
        delta_bias[None, :], log_decay, skip_gain[None, :], queries, key_heads, values, out_proj.T, residual,
    )
    copies = [pltpu.VMEM(a.shape, a.dtype) for i, a in enumerate(operands) if i != 13]
    states = pltpu.VMEM((16, 16, 128), F32)
    by_token = pltpu.VMEM((2048, 128), F32)
    return pl.pallas_call(
        block_kernel,
        out_shape=(
            jax.ShapeDtypeStruct(x_stream.shape, BF), jax.ShapeDtypeStruct(residual.shape, BF)
        ),
        in_specs=[pl.BlockSpec(memory_space=pl.ANY)] * 15,
        out_specs=(pl.BlockSpec(memory_space=pltpu.VMEM),) * 2,
        scratch_shapes=copies + [
            pltpu.VMEM((2, 128, 512), BF),
            pltpu.VMEM((256, 128), BF),
            pltpu.VMEM((128, 1024), BF),
            pltpu.VMEM((4, 8, 256, 128), BF),
            pltpu.VMEM((4, 8, 128, 256), BF),
            pltpu.VMEM((4, 8, LOW, 1024), BF),
            pltpu.VMEM((8, 4, 64 - LOW, 1024), BF),
            pltpu.VMEM((1, 1024), F32),
            pltpu.VMEM((1, 1024), F32),
            pltpu.VMEM((128, 1024), F32),
            pltpu.VMEM((1024, 256), BF),
            pltpu.VMEM((4, 2, 8, 64 - LOW, 128), BF),
            pltpu.VMEM((4, 2, 8, 64 - LOW, 128), BF),
            pltpu.VMEM((4, 2, 8, LOW, 128), BF),
            pltpu.VMEM((4, 2, 8, LOW, 128), BF),
            pltpu.VMEM((1024, 128), F32),
            pltpu.VMEM((16, 2048), BF),
            pltpu.VMEM((136, 2048), F32),
            pltpu.VMEM((128, 2048), BF),
            pltpu.VMEM((128, 256), BF),
            pltpu.VMEM((32, 128), F32),
            pltpu.VMEM((3, 128, 256), BF),
            pltpu.VMEM((3, 32, 128), F32),
            pltpu.VMEM((32, 128), F32),
            pltpu.SMEM((32, 128), F32),
            by_token, by_token, by_token,
            pltpu.VMEM((256, 128), F32),
            pltpu.VMEM((16, 2, 16, 128), BF),
            pltpu.VMEM((16, 2, 16, 128), BF),
            states, states,
            pltpu.VMEM((2, 16, 128), F32),
            pltpu.VMEM((3, 2, 16, 128), F32),
            pltpu.VMEM((16, 16, 128), BF),
            pltpu.VMEM((16, 16, 128), BF),
            dma((16,)), dma((4,)), dma((4,)), dma((3, 4, 8)), dma((3, 4, 8)), dma((8, 4)), dma((8, 4)),
            dma((2,)), dma((2,)), dma((4, 2, 6)), dma((4, 2, 6)), dma((1,)), dma((1,)),
            dma((2, 4)), dma((2, 4)), dma((16,)), dma((16,)), dma((4,)), dma((4,)),
            dma((16,)), dma((16,)),
        ],
        compiler_params=pltpu.CompilerParams(
            collective_id=0, has_side_effects=True, vmem_limit_bytes=56 * 1024 * 1024
        ),
    )(*operands)


def solution(mesh):
    both = P("ctx", "tp")
    placed = (
        both, both, P(None, "tp"), P("tp"), P("tp", None), P(None, "tp"), P(None, "tp"), P("tp"),
        P(None, "tp"), P("tp"), both, both, both, P("tp", "ctx"), both,
    )
    return jax.shard_map(
        block, mesh=mesh, in_specs=placed, out_specs=(both, both), check_vma=False
    )
```

```python
import math

import jax
import jax.numpy as jnp
from jax import lax
from jax.experimental import pallas as pl
from jax.experimental.pallas import tpu as pltpu
from jax.sharding import PartitionSpec as P

HD = 128
NS = 16
BF = jnp.bfloat16
F32 = jnp.float32
MESH = pl.DeviceIdType.MESH
LOG2E = math.log2(math.e)
SCALE = LOG2E / math.sqrt(HD)
X_OFFSET = (0, 3, 1, 2)
WIDE = 512
LOW = 16
GROUPS = ((0, 1), (1, 2), (3, 2), (5, 2), (7, 1))


def at(ctx, tp):
    return {"ctx": ctx, "tp": tp}


def remote(src, dst, send, recv, peer):
    return pltpu.make_async_remote_copy(
        src_ref=src, dst_ref=dst, send_sem=send, recv_sem=recv, device_id=peer, device_id_type=MESH
    )


def block_kernel(
    x_hbm, z_hbm, ck_hbm, cb_hbm, dd_hbm, sp_hbm, du_hbm, db_hbm, ld_hbm, sg_hbm,
    q_hbm, k_hbm, v_hbm, wt_hbm, res_hbm, mix_ref, out_ref,
    x_ref, z_ref, ck_ref, cb_ref, dd_ref, sp_ref, du_ref, db_ref, ld_ref, sg_ref,
    q_ref, k_ref, v_ref, res_ref,
    qts, vts, qt, kbuf, vtbuf, wlow, wbuf, m_ref, l_ref, acc, att, stage, landed, stage_low, landed_low, out_t,
    rim, padded, act, dpart, gpart, dland, gland, gsum, gates, steps, inject, scanned, decay,
    ends, ends_in, before, shift, column, column_in, entry_out, entry,
    load_sem, pair_send, pair_recv, kv_send, kv_recv, w_send, w_recv, half_send, half_recv,
    y_send, y_recv, rim_send, rim_recv, tp_send, tp_recv, col_send, col_recv, x_send, x_recv,
    back_send, back_recv,
):
    me = lax.axis_index("ctx")
    y = lax.axis_index("tp")
    core = me % 2
    other = 1 - core
    chip = me // 2
    z = chip % 8
    x = me // 16
    k = me % 16
    partner = at(me + 1 - 2 * core, y)
    after = at((me + 1) % 64, y)
    earlier = at((me + 63) % 64, y)
    right_z = at(x * 16 + ((z + 1) % 8) * 2 + core, y)
    left_z = at(x * 16 + ((z + 7) % 8) * 2 + core, y)
    right_x = at(((x + 1) % 4) * 16 + k, y)
    left_x = at(((x + 3) % 4) * 16 + k, y)

    def col_peer(gap):
        return at(x * 16 + (k + gap) % 16, y)

    def x_peer(gap):
        return at(((x + gap) % 4) * 16 + k, y)

    barrier = pltpu.get_barrier_semaphore()

    def greet(peer):
        pl.semaphore_signal(barrier, inc=1, device_id=peer, device_id_type=MESH)

    greet(after)
    greet(earlier)
    for gap in (1, 2, 3):
        greet(x_peer(gap))
        for r in range(2):
            greet(at(chip * 2 + r, (y + gap) % 4))
    for gap in range(1, 16):
        greet(col_peer(gap))

    loads = {}
    pairs = (
        ("v", v_hbm, v_ref), ("k", k_hbm, k_ref), ("w", wt_hbm.at[pl.ds(LOW, 64 - LOW)], wbuf.at[0, 0]), ("wl", wt_hbm.at[pl.ds(0, LOW)], wlow.at[0, 0]), ("q", q_hbm, q_ref),
        ("x", x_hbm, x_ref), ("ck", ck_hbm, ck_ref), ("cb", cb_hbm, cb_ref), ("dd", dd_hbm, dd_ref),
        ("sp", sp_hbm, sp_ref), ("ld", ld_hbm, ld_ref), ("du", du_hbm, du_ref), ("db", db_hbm, db_ref),
        ("z", z_hbm, z_ref), ("sg", sg_hbm, sg_ref), ("res", res_hbm, res_ref),
    )
    for i, (name, src, dst) in enumerate(pairs):
        loads[name] = pltpu.make_async_copy(src, dst, load_sem.at[i])
        loads[name].start()

    loads["v"].wait()
    vts[...] = v_ref[...].astype(F32).T.astype(BF)
    loads["q"].wait()
    for g in range(2):
        for h in range(4):
            head = q_ref[:, (g * 4 + h) * HD:(g * 4 + h + 1) * HD]
            qts[g, :, h * HD:(h + 1) * HD] = head.astype(F32).T.astype(BF)
    m_ref[...] = jnp.full_like(m_ref, -1e30)
    l_ref[...] = jnp.zeros_like(l_ref)
    acc[...] = jnp.zeros_like(acc)

    def convolve(count):
        for c in range(8):
            cols = slice(c * 256, (c + 1) * 256)
            conv = cb_ref[:, cols]
            for tap in range(4):
                conv = conv + ck_ref[tap:tap + 1, cols] * padded[5 + tap:5 + tap + count, cols]
            act[:count, cols] = (conv / (1.0 + jnp.exp(-conv))).astype(BF)

    loads["x"].wait()
    loads["ck"].wait()
    loads["cb"].wait()
    padded[:8, :] = jnp.zeros((8, 2048), F32)
    padded[8:, :] = x_ref[...].astype(F32)
    convolve(128)
    loads["ld"].wait()
    rate = -LOG2E * jnp.exp(ld_ref[...])
    for j in range(16):
        decay[pl.ds(j, 16, stride=16), :] = rate[:, j * 128:(j + 1) * 128]
    loads["k"].wait()
    loads["w"].wait()
    loads["wl"].wait()
    pl.semaphore_wait(barrier, 26)

    own_rows = pl.ds(pl.multiple_of(core * 128, 128), 128)
    other_rows = pl.ds(pl.multiple_of(other * 128, 128), 128)
    own_cols = pl.ds(pl.multiple_of(core * 512, 512), 512)

    def pair_copy(src, dst, i):
        return remote(src, dst, pair_send.at[i], pair_recv.at[i], partner)

    swaps = (
        pair_copy(k_ref.at[:, other_rows], kbuf.at[0, 0, own_rows, :], 0),
        pair_copy(vts.at[other_rows, :], vtbuf.at[0, 0, :, own_rows], 1),
        pair_copy(qts.at[other], qt.at[:, own_cols], 2),
    )
    for swap in swaps:
        swap.start()

    bufs = (kbuf, vtbuf, wlow)

    def kv_copy(kind, src, dst, peer):
        return remote(
            bufs[kind].at[src], bufs[kind].at[dst], kv_send.at[(kind, *dst)], kv_recv.at[(kind, *dst)], peer
        )

    def kv_arrived(kind, slot):
        kv_copy(kind, slot, slot, right_z).wait_recv()

    def spread_x(kind, zs):
        kv_copy(kind, (0, zs), (1, zs), right_x).start()
        kv_copy(kind, (0, zs), (2, zs), left_x).start()

    def w_copy(src, dst, peer):
        return remote(wbuf.at[src], wbuf.at[dst], w_send.at[dst], w_recv.at[dst], peer)

    def w_arrived(slot):
        w_copy(slot, slot, right_z).wait_recv()

    def half_copy(source, rows, i, peer):
        half = pl.ds(rows, 32 - rows // 2)
        return remote(
            wbuf.at[0, source, half, :], wbuf.at[0, 3, half, :], half_send.at[i], half_recv.at[i], peer
        )

    def w_spread_z(xs):
        w_copy((0, xs), (1, xs), right_z).start()
        w_copy((0, xs), (2, xs), left_z).start()

    w_copy((0, 0), (0, 1), right_x).start()
    w_copy((0, 0), (0, 2), left_x).start()
    kbuf[0, 0, own_rows, :] = k_ref[:, own_rows]
    vtbuf[0, 0, :, own_rows] = vts[own_rows, :]
    rim_copy = remote(x_ref.at[pl.ds(112, 16), :], rim, rim_send.at[0], rim_recv.at[0], after)
    rim_copy.start()
    qt[:, own_cols] = qts[core]
    for kind in (0, 1):
        swaps[kind].wait()
        kv_copy(kind, (0, 0), (0, 1), right_z).start()
        kv_copy(kind, (0, 0), (0, 2), left_z).start()
        spread_x(kind, 0)
    w_spread_z(0)

    def low_hop(h):
        if h == 0:
            kv_copy(2, (0, 0), (0, 1), right_z).start()
            kv_copy(2, (0, 0), (0, 2), left_z).start()
        elif h < 4:
            kv_arrived(2, (0, 2 * h - 1))
            kv_copy(2, (0, 2 * h - 1), (0, 2 * h + 1), right_z).start()
            kv_arrived(2, (0, 2 * h))
            if h < 3:
                kv_copy(2, (0, 2 * h), (0, 2 * h + 2), left_z).start()
        else:
            kv_arrived(2, (0, 7))

    def kv_hop(h):
        for kind in (0, 1):
            if h < 4:
                kv_arrived(kind, (0, 2 * h - 1))
                if h < 3:
                    kv_copy(kind, (0, 2 * h - 1), (0, 2 * h + 1), right_z).start()
                elif kind == 0:
                    kv_copy(kind, (0, 5), (0, 7), right_z).start()
                spread_x(kind, 2 * h - 1)
                kv_arrived(kind, (0, 2 * h))
                if h < 3:
                    kv_copy(kind, (0, 2 * h), (0, 2 * h + 2), left_z).start()
                elif kind == 1:
                    kv_copy(kind, (0, 6), (0, 7), left_z).start()
                spread_x(kind, 2 * h)
            else:
                kv_arrived(kind, (0, 7))
                spread_x(kind, 7)

    def attend(slots, biases):
        def scores(j):
            cols = slice(j * WIDE, (j + 1) * WIDE)
            return [jnp.dot(kbuf[slot], qt[:, cols], preferred_element_type=F32) for slot in slots]

        following = scores(0)
        for j in range(1024 // WIDE):
            cols = slice(j * WIDE, (j + 1) * WIDE)
            now = following
            if (j + 1) * WIDE < 1024:
                following = scores(j + 1)
            if biases is None:
                key = lax.broadcasted_iota(jnp.int32, (256, WIDE), 0)
                row = lax.broadcasted_iota(jnp.int32, (256, WIDE), 1) % 128 + (j * WIDE // 512) * 128
                now = [jnp.where(key <= row, s, -1e30) for s in now]
            m_old = m_ref[:, cols]
            m_new = m_old
            for i, s in enumerate(now):
                top = jnp.max(s, axis=0, keepdims=True) * SCALE
                m_new = jnp.maximum(m_new, top if biases is None else top + biases[i])
            alpha = jnp.exp2(m_old - m_new)
            gained = l_ref[:, cols] * alpha
            mixed = acc[:, cols] * alpha
            for i, s in enumerate(now):
                p = jnp.exp2(s * SCALE - (m_new if biases is None else m_new - biases[i]))
                gained = gained + jnp.sum(p, axis=0, keepdims=True)
                mixed = mixed + jnp.dot(vtbuf[slots[i]], p.astype(BF), preferred_element_type=F32)
            m_ref[:, cols] = m_new
            l_ref[:, cols] = gained
            acc[:, cols] = mixed

    def z_of(zs):
        return (z + 8 + (1 - 2 * (zs % 2)) * ((zs + 1) // 2)) % 8

    def attend_earlier(first, second, zs):
        earlier_than = [((x + X_OFFSET[xs]) % 4) * 8 + z_of(zs) < chip for xs in (first, second)]

        @pl.when(earlier_than[0] | earlier_than[1])
        def _():
            attend(
                [(xs, zs) for xs in (first, second)],
                [jnp.where(flag, 0.0, -1e30).astype(F32) for flag in earlier_than],
            )

    swaps[2].wait()
    attend([(0, 0)], None)

    rim_copy.wait()
    padded[:8, :] = jnp.where(me > 0, rim[8:, :].astype(F32), 0.0)
    convolve(16)
    loads["dd"].wait()
    loads["sp"].wait()
    dpart[...] = jnp.dot(act[...], dd_ref[...], preferred_element_type=F32).astype(BF)
    gpart[...] = lax.dot_general(
        sp_ref[...], act[...], (((1,), (1,)), ((), ())), preferred_element_type=F32
    )

    def tp_copies(gap):
        peer = at(me, (y + gap) % 4)
        return (
            remote(dpart, dland.at[gap - 1], tp_send.at[0, gap], tp_recv.at[0, gap], peer),
            remote(gpart, gland.at[gap - 1], tp_send.at[1, gap], tp_recv.at[1, gap], peer),
        )

    for gap in (2, 1, 3):
        for copy in tp_copies(gap):
            copy.start()


    kv_hop(1)
    w_arrived((0, 1))
    half_copy(1, 0, 0, right_x).start()
    w_arrived((0, 2))
    half_copy(2, 32, 1, left_x).start()
    w_spread_z(1)
    low_hop(0)

    def step_stage():
        loads["du"].wait()
        loads["db"].wait()
        for gap in (1, 3, 2):
            for copy in tp_copies(gap):
                copy.wait()
        gsum[...] = gpart[...] + gland[0] + gland[1] + gland[2]
        to_scalars = pltpu.make_async_copy(gsum, gates, load_sem.at[0])
        to_scalars.start()
        low = (
            dpart[...].astype(F32) + dland[0].astype(F32) + dland[1].astype(F32) + dland[2].astype(F32)
        ).astype(BF)
        for c in range(8):
            cols = slice(c * 256, (c + 1) * 256)
            raw = jnp.dot(low, du_ref[:, cols], preferred_element_type=F32) + db_ref[:, cols]
            size = jnp.maximum(raw, 0.0) + jnp.log1p(jnp.exp(-jnp.abs(raw)))
            drive = size * act[:, cols].astype(F32)
            for half in range(2):
                j = c * 2 + half
                steps[pl.ds(j, 128, stride=16), :] = size[:, half * 128:(half + 1) * 128]
                inject[pl.ds(j, 128, stride=16), :] = drive[:, half * 128:(half + 1) * 128]
        to_scalars.wait()

    def rows_of(t):
        return pl.ds(pl.multiple_of(t * 16, 16), 16)

    def first_pass(half):
        base = half * 8
        rates = [decay[(base + n) * 16:(base + n + 1) * 16, :] for n in range(8)]

        def advance(t, carried):
            size = steps[rows_of(t), :]
            drive = inject[rows_of(t), :]
            out = [
                jnp.exp2(rates[n] * size) * carried[n] + gates[base + n, t] * drive
                for n in range(8)
            ]
            return tuple(out) + (carried[8] + size,)

        zero = jnp.zeros((16, 128), F32)
        last = lax.fori_loop(0, 128, advance, (zero,) * 9, unroll=2)
        for n in range(8):
            ends[base + n, 0] = last[n].astype(BF)
            ends[base + n, 1] = last[8].astype(BF)

    def col_copies(gap):
        peer = col_peer(gap)
        return (
            remote(ends.at[(k + gap) % 16], ends_in.at[gap], col_send.at[gap], col_recv.at[gap], peer),
        )

    def col_start(gap, _):
        for copy in col_copies(gap):
            copy.start()
        return 0

    def col_wait(gap, _):
        for copy in col_copies(gap):
            copy.wait()
        return 0

    def ends_stage():
        lax.fori_loop(1, 16, col_start, 0)
        ends_in[0] = ends[k]

    def x_copy(gap):
        return remote(column, column_in.at[gap - 1], x_send.at[gap], x_recv.at[gap], x_peer(gap))

    def column_stage():
        lax.fori_loop(1, 16, col_wait, 0)
        my_rate = decay[rows_of(k), :]

        def chain(j, carried):
            state, sizes = carried
            before[j] = state
            shift[j] = sizes
            slot = (k + 16 - j) % 16
            size = ends_in[slot, 1].astype(F32)
            return (jnp.exp2(my_rate * size) * state + ends_in[slot, 0].astype(F32), sizes + size)

        zero = jnp.zeros((16, 128), F32)
        state, sizes = lax.fori_loop(0, 16, chain, (zero, zero))
        column[0] = state
        column[1] = sizes
        for gap in (2, 1, 3):
            x_copy(gap).start()

    def back_copy(gap):
        return remote(
            entry_out.at[(k + gap) % 16], entry.at[k], back_send.at[gap], back_recv.at[gap], col_peer(gap)
        )

    def back_arrival(gap):
        return remote(
            entry_out.at[(k + gap) % 16], entry.at[(k + 16 - gap) % 16],
            back_send.at[gap], back_recv.at[gap], col_peer(gap),
        )

    def back_start(gap, _):
        back_copy(gap).start()
        return 0

    def back_wait(gap, _):
        back_copy(gap).wait_send()
        back_arrival(gap).wait_recv()
        return 0

    def entry_stage():
        for gap in (1, 3, 2):
            x_copy(gap).wait()
        my_rate = decay[rows_of(k), :]
        incoming = jnp.zeros((16, 128), F32)
        for xs in range(3):
            slot = jnp.minimum((x + 3 - xs) % 4, 2)
            ahead = jnp.exp2(my_rate * column_in[slot, 1]) * incoming + column_in[slot, 0]
            incoming = jnp.where(xs < x, ahead, incoming)

        def finish(j, _):
            entry_out[j] = (before[j] + jnp.exp2(my_rate * shift[j]) * incoming).astype(BF)
            return 0

        lax.fori_loop(0, 16, finish, 0)
        lax.fori_loop(1, 16, back_start, 0)
        entry[k] = entry_out[k]

    def w_event(e):
        h = 1 + e // 4
        xs = e % 4
        w_arrived((2 * h - 1, xs))

        @pl.when((h < 3) | (xs < 2))
        def _():
            w_copy((2 * h - 1, xs), (2 * h + 1, xs), right_z).start()

        w_arrived((2 * h, xs))

        @pl.when(h < 3)
        def _():
            w_copy((2 * h, xs), (2 * h + 2, xs), left_z).start()

        @pl.when((h == 3) & (xs >= 2))
        def _():
            w_copy((2 * h, xs), (7, xs), left_z).start()

    def low_spread(zs, _):
        spread_x(2, zs)
        return 0

    def sweep(i, _):
        @pl.when(i == 1)
        def _():
            kv_hop(2)
            low_hop(1)
            w_spread_z(2)

        @pl.when(i == 2)
        def _():
            kv_hop(3)
            low_hop(2)
            half_copy(1, 0, 0, right_x).wait_recv()
            half_copy(2, 32, 1, left_x).wait_recv()
            w_spread_z(3)

        @pl.when(i == 3)
        def _():
            kv_hop(4)
            low_hop(3)

        for kind, near, peer in ((0, 1, right_x), (1, 2, left_x)):
            kv_arrived(kind, (1, i))
            kv_arrived(kind, (2, i))
            kv_copy(kind, (near, i), (3, i), peer).start()

        @pl.when(i == 6)
        def _():
            lax.fori_loop(0, 4, low_spread, 0)

        @pl.when(i == 7)
        def _():
            low_hop(4)
            lax.fori_loop(4, 8, low_spread, 0)

        @pl.when(i >= 2)
        def _():
            w_event(i - 2 + i // 7)

        attend_earlier(1, 2, i)

        @pl.when(i == 6)
        def _():
            w_event(5)

        @pl.when(i == 0)
        def _():
            step_stage()

        @pl.when(i == 1)
        def _():
            first_pass(0)

        @pl.when(i == 2)
        def _():
            first_pass(1)
            ends_stage()

        @pl.when(i > 0)
        def _():
            for kind in (0, 1):
                kv_arrived(kind, (3, i - 1))
            attend_earlier(0, 3, i - 1)

        @pl.when(i == 4)
        def _():
            column_stage()

        @pl.when(i == 6)
        def _():
            entry_stage()

        return 0

    lax.fori_loop(0, 8, sweep, 0)
    for kind in (0, 1):
        kv_arrived(kind, (3, 7))
    attend_earlier(0, 3, 7)

    inverse = 1.0 / l_ref[...]
    heads = []
    for h in range(4):
        pieces = []
        for r in range(2):
            cols = slice(r * 512 + h * 128, r * 512 + (h + 1) * 128)
            pieces.append((acc[:, cols] * inverse[:, cols]).astype(BF))
        heads.append(jnp.concatenate(pieces, axis=1))
    att[own_cols, :] = jnp.concatenate(heads, axis=0)
    att_swap = pair_copy(att.at[own_cols, :], att.at[own_cols, :], 3)
    att_swap.start()
    lax.fori_loop(1, 16, back_wait, 0)

    def second_pass(half):
        base = half * 8
        rates = [decay[(base + n) * 16:(base + n + 1) * 16, :] for n in range(8)]

        def advance(t, carried):
            size = steps[rows_of(t), :]
            drive = inject[rows_of(t), :]
            out = []
            mixed = scanned[rows_of(t), :] if half else None
            for n in range(8):
                state = jnp.exp2(rates[n] * size) * carried[n] + gates[base + n, t] * drive
                term = gates[NS + base + n, t] * state
                mixed = term if mixed is None else mixed + term
                out.append(state)
            scanned[rows_of(t), :] = mixed
            return tuple(out)

        lax.fori_loop(0, 128, advance, tuple(entry[base + n].astype(F32) for n in range(8)), unroll=2)

    def slot_of(gap):
        d = (y + gap + 4 - x) % 4
        return 2 * d - d // 2 - 4 * (d // 3)

    def y_copy(gap, r, g):
        first, count = GROUPS[g]
        rows = pl.ds(first, count)
        return remote(
            stage.at[slot_of(gap), r, rows], landed.at[gap, core, rows],
            y_send.at[gap, r, g], y_recv.at[gap, core, g], at(chip * 2 + r, (y + gap) % 4),
        )

    def y_arrival(gap, c, g):
        first, count = GROUPS[g]
        rows = pl.ds(first, count)
        return remote(
            stage.at[0, 0, rows], landed.at[gap, c, rows],
            y_send.at[gap, c, g], y_recv.at[gap, c, g], partner,
        )

    def project(g):
        first, count = GROUPS[g]
        for zs in range(first, first + count):
            part = jnp.dot(
                wbuf[zs].reshape(4 * (64 - LOW), 1024), att[...], preferred_element_type=F32
            ).astype(BF)
            for xs in range(4):
                for r in range(2):
                    stage[xs, r, zs] = part[xs * (64 - LOW):(xs + 1) * (64 - LOW), r * 128:(r + 1) * 128]
        for gap in (2, 1, 3):
            for r in range(2):
                y_copy(gap, r, g).start()
        y_copy_partner(g).start()
        for zs in range(first, first + count):
            landed[0, core, zs] = stage[slot_of(0), core, zs]

    def y_copy_partner(g):
        first, count = GROUPS[g]
        rows = pl.ds(first, count)
        return remote(
            stage.at[slot_of(0), other, rows], landed.at[0, core, rows],
            y_send.at[0, 0, g], y_recv.at[0, core, g], partner,
        )

    def low_cross(i, _):
        for zs, near, peer in ((2 * i, 1, right_x), (2 * i + 1, 2, left_x)):
            kv_arrived(2, (1, zs))
            kv_arrived(2, (2, zs))
            kv_copy(2, (near, zs), (3, zs), peer).start()
        return 0

    def y_low(gap, r):
        return remote(
            stage_low.at[slot_of(gap), r], landed_low.at[gap, core],
            y_send.at[gap, r, 5], y_recv.at[gap, core, 5], at(chip * 2 + r, (y + gap) % 4),
        )

    def y_low_partner():
        return remote(
            stage_low.at[slot_of(0), other], landed_low.at[0, core],
            y_send.at[0, 0, 5], y_recv.at[0, core, 5], partner,
        )

    def y_low_arrival(gap, c):
        return remote(
            stage_low.at[0, 0], landed_low.at[gap, c], y_send.at[gap, c, 5], y_recv.at[gap, c, 5], partner
        )

    def project_low():
        for zs in range(8):
            kv_arrived(2, (3, zs))
        for xs in range(4):
            part = jnp.dot(
                wlow[xs].reshape(8 * LOW, 1024), att[...], preferred_element_type=F32
            ).astype(BF)
            for r in range(2):
                stage_low[xs, r] = part[:, r * 128:(r + 1) * 128].reshape(8, LOW, 128)
        for gap in (2, 1, 3):
            for r in range(2):
                y_low(gap, r).start()
        y_low_partner().start()
        landed_low[0, core] = stage_low[slot_of(0), core]

    w_event(7)
    att_swap.wait()
    project(0)
    project(1)
    w_event(8)
    lax.fori_loop(0, 2, low_cross, 0)
    project(2)
    w_event(9)
    lax.fori_loop(2, 4, low_cross, 0)
    w_event(10)
    second_pass(0)
    w_event(11)
    project(3)
    project_low()
    for xs in range(4):
        w_arrived((7, xs))
    project(4)
    second_pass(1)
    loads["z"].wait()
    loads["sg"].wait()
    for j in range(16):
        cols = slice(j * 128, (j + 1) * 128)
        gate = z_ref[:, cols].astype(F32)
        mixed = scanned[pl.ds(j, 128, stride=16), :] + sg_ref[:, cols] * act[:, cols].astype(F32)
        mix_ref[:, cols] = (mixed * (gate / (1.0 + jnp.exp(-gate)))).astype(BF)

    for i in range(2):
        half_copy(i + 1, 32 * i, i, right_x).wait_send()
    w_copy((0, 0), (0, 1), right_x).wait_send()
    w_copy((0, 0), (0, 2), left_x).wait_send()

    def drain(zs, _):
        for kind in (0, 1, 2):
            @pl.when((zs > 0) & (zs < 7))
            def _():
                kv_copy(kind, (0, zs), (0, zs), right_z).wait_send()

            for xs in range(1, 4):
                kv_copy(kind, (xs, zs), (xs, zs), right_z).wait_send()

        @pl.when(zs > 0)
        def _():
            for xs in range(4):
                w_copy((zs, xs), (zs, xs), right_z).wait_send()

        return 0

    lax.fori_loop(0, 8, drain, 0)
    for kind in (0, 1, 2):
        kv_copy(kind, (0, 7), (0, 7), right_z).wait_send()
    loads["res"].wait()
    for g in range(5):
        y_copy_partner(g).wait_send()
        for gap in (1, 2, 3):
            for r in range(2):
                y_copy(gap, r, g).wait_send()
        y_arrival(0, other, g).wait_recv()
        for gap in (1, 3, 2):
            for c in range(2):
                y_arrival(gap, c, g).wait_recv()
        first, count = GROUPS[g]
        for zs in range(first, first + count):
            for c in range(2):
                part = landed[0, c, zs].astype(F32)
                for gap in range(1, 4):
                    part = part + landed[gap, c, zs].astype(F32)
                rows = pl.ds(pl.multiple_of(z_of(zs) * 128 + c * 64 + LOW, LOW), 64 - LOW)
                out_t[rows, :] = part
    y_low_partner().wait_send()
    for gap in (1, 2, 3):
        for r in range(2):
            y_low(gap, r).wait_send()
    y_low_arrival(0, other).wait_recv()
    for gap in (1, 3, 2):
        for c in range(2):
            y_low_arrival(gap, c).wait_recv()
    for zs in range(8):
        for c in range(2):
            part = landed_low[0, c, zs].astype(F32)
            for gap in range(1, 4):
                part = part + landed_low[gap, c, zs].astype(F32)
            rows = pl.ds(pl.multiple_of(z_of(zs) * 128 + c * 64, 64), LOW)
            out_t[rows, :] = part
    for zo in range(8):
        cols = slice(zo * 128, (zo + 1) * 128)
        out_ref[:, cols] = (res_ref[:, cols].astype(F32) + out_t[cols, :].T).astype(BF)


def block(
    x_stream, z_stream, conv_kernel, conv_bias, delta_down, state_proj, delta_up, delta_bias,
    log_decay, skip_gain, queries, key_heads, values, out_proj, residual,
):
    dma = pltpu.SemaphoreType.DMA
    operands = (
        x_stream, z_stream, conv_kernel, conv_bias[None, :], delta_down, state_proj, delta_up,
        delta_bias[None, :], log_decay, skip_gain[None, :], queries, key_heads, values, out_proj.T, residual,
    )
    copies = [pltpu.VMEM(a.shape, a.dtype) for i, a in enumerate(operands) if i != 13]
    states = pltpu.VMEM((16, 16, 128), F32)
    by_token = pltpu.VMEM((2048, 128), F32)
    return pl.pallas_call(
        block_kernel,
        out_shape=(
            jax.ShapeDtypeStruct(x_stream.shape, BF), jax.ShapeDtypeStruct(residual.shape, BF)
        ),
        in_specs=[pl.BlockSpec(memory_space=pl.ANY)] * 15,
        out_specs=(pl.BlockSpec(memory_space=pltpu.VMEM),) * 2,
        scratch_shapes=copies + [
            pltpu.VMEM((2, 128, 512), BF),
            pltpu.VMEM((256, 128), BF),
            pltpu.VMEM((128, 1024), BF),
            pltpu.VMEM((4, 8, 256, 128), BF),
            pltpu.VMEM((4, 8, 128, 256), BF),
            pltpu.VMEM((4, 8, LOW, 1024), BF),
            pltpu.VMEM((8, 4, 64 - LOW, 1024), BF),
            pltpu.VMEM((1, 1024), F32),
            pltpu.VMEM((1, 1024), F32),
            pltpu.VMEM((128, 1024), F32),
            pltpu.VMEM((1024, 256), BF),
            pltpu.VMEM((4, 2, 8, 64 - LOW, 128), BF),
            pltpu.VMEM((4, 2, 8, 64 - LOW, 128), BF),
            pltpu.VMEM((4, 2, 8, LOW, 128), BF),
            pltpu.VMEM((4, 2, 8, LOW, 128), BF),
            pltpu.VMEM((1024, 128), F32),
            pltpu.VMEM((16, 2048), BF),
            pltpu.VMEM((136, 2048), F32),
            pltpu.VMEM((128, 2048), BF),
            pltpu.VMEM((128, 256), BF),
            pltpu.VMEM((32, 128), F32),
            pltpu.VMEM((3, 128, 256), BF),
            pltpu.VMEM((3, 32, 128), F32),
            pltpu.VMEM((32, 128), F32),
            pltpu.SMEM((32, 128), F32),
            by_token, by_token, by_token,
            pltpu.VMEM((256, 128), F32),
            pltpu.VMEM((16, 2, 16, 128), BF),
            pltpu.VMEM((16, 2, 16, 128), BF),
            states, states,
            pltpu.VMEM((2, 16, 128), F32),
            pltpu.VMEM((3, 2, 16, 128), F32),
            pltpu.VMEM((16, 16, 128), BF),
            pltpu.VMEM((16, 16, 128), BF),
            dma((16,)), dma((4,)), dma((4,)), dma((3, 4, 8)), dma((3, 4, 8)), dma((8, 4)), dma((8, 4)),
            dma((2,)), dma((2,)), dma((4, 2, 6)), dma((4, 2, 6)), dma((1,)), dma((1,)),
            dma((2, 4)), dma((2, 4)), dma((16,)), dma((16,)), dma((4,)), dma((4,)),
            dma((16,)), dma((16,)),
        ],
        compiler_params=pltpu.CompilerParams(
            collective_id=0, has_side_effects=True, vmem_limit_bytes=56 * 1024 * 1024
        ),
    )(*operands)


def solution(mesh):
    both = P("ctx", "tp")
    placed = (
        both, both, P(None, "tp"), P("tp"), P("tp", None), P(None, "tp"), P(None, "tp"), P("tp"),
        P(None, "tp"), P("tp"), both, both, both, P("tp", "ctx"), both,
    )
    return jax.shard_map(
        block, mesh=mesh, in_specs=placed, out_specs=(both, both), check_vma=False
    )
```

```python
import math

import jax
import jax.numpy as jnp
from jax import lax
from jax.experimental import pallas as pl
from jax.experimental.pallas import tpu as pltpu
from jax.sharding import PartitionSpec as P

HD = 128
NS = 16
BF = jnp.bfloat16
F32 = jnp.float32
MESH = pl.DeviceIdType.MESH
LOG2E = math.log2(math.e)
SCALE = LOG2E / math.sqrt(HD)
X_OFFSET = (0, 3, 1, 2)
WIDE = 512
LOW = 16
GROUPS = ((0, 1), (1, 2), (3, 2), (5, 2), (7, 1))


def at(ctx, tp):
    return {"ctx": ctx, "tp": tp}


def remote(src, dst, send, recv, peer):
    return pltpu.make_async_remote_copy(
        src_ref=src, dst_ref=dst, send_sem=send, recv_sem=recv, device_id=peer, device_id_type=MESH
    )


def block_kernel(
    x_hbm, z_hbm, ck_hbm, cb_hbm, dd_hbm, sp_hbm, du_hbm, db_hbm, ld_hbm, sg_hbm,
    q_hbm, k_hbm, v_hbm, wt_hbm, res_hbm, mix_ref, out_ref,
    x_ref, z_ref, ck_ref, cb_ref, dd_ref, sp_ref, du_ref, db_ref, ld_ref, sg_ref,
    q_ref, k_ref, v_ref, res_ref,
    qts, vts, qt, kbuf, vtbuf, wlow, wbuf, m_ref, l_ref, acc, att, stage, landed, stage_low, landed_low, out_t,
    rim, padded, act, dpart, gpart, dland, gland, gsum, gates, steps, inject, scanned, decay,
    ends, ends_in, before, shift, column, column_in, entry_out, entry,
    load_sem, pair_send, pair_recv, kv_send, kv_recv, w_send, w_recv, half_send, half_recv,
    y_send, y_recv, rim_send, rim_recv, tp_send, tp_recv, col_send, col_recv, x_send, x_recv,
    back_send, back_recv,
):
    me = lax.axis_index("ctx")
    y = lax.axis_index("tp")
    core = me % 2
    other = 1 - core
    chip = me // 2
    z = chip % 8
    x = me // 16
    k = me % 16
    partner = at(me + 1 - 2 * core, y)
    after = at((me + 1) % 64, y)
    earlier = at((me + 63) % 64, y)
    right_z = at(x * 16 + ((z + 1) % 8) * 2 + core, y)
    left_z = at(x * 16 + ((z + 7) % 8) * 2 + core, y)
    right_x = at(((x + 1) % 4) * 16 + k, y)
    left_x = at(((x + 3) % 4) * 16 + k, y)

    def col_peer(gap):
        return at(x * 16 + (k + gap) % 16, y)

    def x_peer(gap):
        return at(((x + gap) % 4) * 16 + k, y)

    barrier = pltpu.get_barrier_semaphore()

    def greet(peer):
        pl.semaphore_signal(barrier, inc=1, device_id=peer, device_id_type=MESH)

    for peer in (partner, after, earlier, right_z, left_z, right_x, left_x):
        greet(peer)
    for gap in (1, 2, 3):
        greet(at(me, (y + gap) % 4))

    loads = {}
    pairs = (
        ("v", v_hbm, v_ref), ("k", k_hbm, k_ref), ("w", wt_hbm.at[pl.ds(LOW, 64 - LOW)], wbuf.at[0, 0]), ("wl", wt_hbm.at[pl.ds(0, LOW)], wlow.at[0, 0]), ("q", q_hbm, q_ref),
        ("x", x_hbm, x_ref), ("ck", ck_hbm, ck_ref), ("cb", cb_hbm, cb_ref), ("dd", dd_hbm, dd_ref),
        ("sp", sp_hbm, sp_ref), ("ld", ld_hbm, ld_ref), ("du", du_hbm, du_ref), ("db", db_hbm, db_ref),
        ("z", z_hbm, z_ref), ("sg", sg_hbm, sg_ref), ("res", res_hbm, res_ref),
    )
    for i, (name, src, dst) in enumerate(pairs):
        loads[name] = pltpu.make_async_copy(src, dst, load_sem.at[i])
        loads[name].start()

    loads["v"].wait()
    vts[...] = v_ref[...].astype(F32).T.astype(BF)
    loads["q"].wait()
    for g in range(2):
        for h in range(4):
            head = q_ref[:, (g * 4 + h) * HD:(g * 4 + h + 1) * HD]
            qts[g, :, h * HD:(h + 1) * HD] = head.astype(F32).T.astype(BF)
    m_ref[...] = jnp.full_like(m_ref, -1e30)
    l_ref[...] = jnp.zeros_like(l_ref)
    acc[...] = jnp.zeros_like(acc)

    def convolve(count):
        for c in range(8):
            cols = slice(c * 256, (c + 1) * 256)
            conv = cb_ref[:, cols]
            for tap in range(4):
                conv = conv + ck_ref[tap:tap + 1, cols] * padded[5 + tap:5 + tap + count, cols]
            act[:count, cols] = (conv / (1.0 + jnp.exp(-conv))).astype(BF)

    loads["x"].wait()
    loads["ck"].wait()
    loads["cb"].wait()
    padded[:8, :] = jnp.zeros((8, 2048), F32)
    padded[8:, :] = x_ref[...].astype(F32)
    convolve(128)
    loads["ld"].wait()
    rate = -LOG2E * jnp.exp(ld_ref[...])
    for j in range(16):
        decay[pl.ds(j, 16, stride=16), :] = rate[:, j * 128:(j + 1) * 128]
    loads["k"].wait()
    loads["w"].wait()
    loads["wl"].wait()
    pl.semaphore_wait(barrier, 10)

    own_rows = pl.ds(pl.multiple_of(core * 128, 128), 128)
    other_rows = pl.ds(pl.multiple_of(other * 128, 128), 128)
    own_cols = pl.ds(pl.multiple_of(core * 512, 512), 512)

    def pair_copy(src, dst, i):
        return remote(src, dst, pair_send.at[i], pair_recv.at[i], partner)

    swaps = (
        pair_copy(k_ref.at[:, other_rows], kbuf.at[0, 0, own_rows, :], 0),
        pair_copy(vts.at[other_rows, :], vtbuf.at[0, 0, :, own_rows], 1),
        pair_copy(qts.at[other], qt.at[:, own_cols], 2),
    )
    for swap in swaps:
        swap.start()

    bufs = (kbuf, vtbuf, wlow)

    def kv_copy(kind, src, dst, peer):
        return remote(
            bufs[kind].at[src], bufs[kind].at[dst], kv_send.at[(kind, *dst)], kv_recv.at[(kind, *dst)], peer
        )

    def kv_arrived(kind, slot):
        kv_copy(kind, slot, slot, right_z).wait_recv()

    def spread_x(kind, zs):
        kv_copy(kind, (0, zs), (1, zs), right_x).start()
        kv_copy(kind, (0, zs), (2, zs), left_x).start()

    def w_copy(src, dst, peer):
        return remote(wbuf.at[src], wbuf.at[dst], w_send.at[dst], w_recv.at[dst], peer)

    def w_arrived(slot):
        w_copy(slot, slot, right_z).wait_recv()

    def half_copy(source, rows, i, peer):
        half = pl.ds(rows, 32 - rows // 2)
        return remote(
            wbuf.at[0, source, half, :], wbuf.at[0, 3, half, :], half_send.at[i], half_recv.at[i], peer
        )

    def w_spread_z(xs):
        w_copy((0, xs), (1, xs), right_z).start()
        w_copy((0, xs), (2, xs), left_z).start()

    w_copy((0, 0), (0, 1), right_x).start()
    w_copy((0, 0), (0, 2), left_x).start()
    kbuf[0, 0, own_rows, :] = k_ref[:, own_rows]
    vtbuf[0, 0, :, own_rows] = vts[own_rows, :]
    rim_copy = remote(x_ref.at[pl.ds(112, 16), :], rim, rim_send.at[0], rim_recv.at[0], after)
    rim_copy.start()
    qt[:, own_cols] = qts[core]
    for kind in (0, 1):
        swaps[kind].wait()
        kv_copy(kind, (0, 0), (0, 1), right_z).start()
        kv_copy(kind, (0, 0), (0, 2), left_z).start()
        spread_x(kind, 0)
    w_spread_z(0)

    def low_hop(h):
        if h == 0:
            kv_copy(2, (0, 0), (0, 1), right_z).start()
            kv_copy(2, (0, 0), (0, 2), left_z).start()
        elif h < 4:
            kv_arrived(2, (0, 2 * h - 1))
            kv_copy(2, (0, 2 * h - 1), (0, 2 * h + 1), right_z).start()
            kv_arrived(2, (0, 2 * h))
            if h < 3:
                kv_copy(2, (0, 2 * h), (0, 2 * h + 2), left_z).start()
        else:
            kv_arrived(2, (0, 7))

    def kv_hop(h):
        for kind in (0, 1):
            if h < 4:
                kv_arrived(kind, (0, 2 * h - 1))
                if h < 3:
                    kv_copy(kind, (0, 2 * h - 1), (0, 2 * h + 1), right_z).start()
                elif kind == 0:
                    kv_copy(kind, (0, 5), (0, 7), right_z).start()
                spread_x(kind, 2 * h - 1)
                kv_arrived(kind, (0, 2 * h))
                if h < 3:
                    kv_copy(kind, (0, 2 * h), (0, 2 * h + 2), left_z).start()
                elif kind == 1:
                    kv_copy(kind, (0, 6), (0, 7), left_z).start()
                spread_x(kind, 2 * h)
            else:
                kv_arrived(kind, (0, 7))
                spread_x(kind, 7)

    def attend(slots, biases):
        def scores(j):
            cols = slice(j * WIDE, (j + 1) * WIDE)
            return [jnp.dot(kbuf[slot], qt[:, cols], preferred_element_type=F32) for slot in slots]

        following = scores(0)
        for j in range(1024 // WIDE):
            cols = slice(j * WIDE, (j + 1) * WIDE)
            now = following
            if (j + 1) * WIDE < 1024:
                following = scores(j + 1)
            if biases is None:
                key = lax.broadcasted_iota(jnp.int32, (256, WIDE), 0)
                row = lax.broadcasted_iota(jnp.int32, (256, WIDE), 1) % 128 + (j * WIDE // 512) * 128
                now = [jnp.where(key <= row, s, -1e30) for s in now]
            m_old = m_ref[:, cols]
            m_new = m_old
            for i, s in enumerate(now):
                top = jnp.max(s, axis=0, keepdims=True) * SCALE
                m_new = jnp.maximum(m_new, top if biases is None else top + biases[i])
            alpha = jnp.exp2(m_old - m_new)
            gained = l_ref[:, cols] * alpha
            mixed = acc[:, cols] * alpha
            for i, s in enumerate(now):
                p = jnp.exp2(s * SCALE - (m_new if biases is None else m_new - biases[i]))
                gained = gained + jnp.sum(p, axis=0, keepdims=True)
                mixed = mixed + jnp.dot(vtbuf[slots[i]], p.astype(BF), preferred_element_type=F32)
            m_ref[:, cols] = m_new
            l_ref[:, cols] = gained
            acc[:, cols] = mixed

    def z_of(zs):
        return (z + 8 + (1 - 2 * (zs % 2)) * ((zs + 1) // 2)) % 8

    def attend_earlier(first, second, zs):
        earlier_than = [((x + X_OFFSET[xs]) % 4) * 8 + z_of(zs) < chip for xs in (first, second)]

        @pl.when(earlier_than[0] | earlier_than[1])
        def _():
            attend(
                [(xs, zs) for xs in (first, second)],
                [jnp.where(flag, 0.0, -1e30).astype(F32) for flag in earlier_than],
            )

    swaps[2].wait()
    attend([(0, 0)], None)

    rim_copy.wait()
    padded[:8, :] = jnp.where(me > 0, rim[8:, :].astype(F32), 0.0)
    convolve(16)
    loads["dd"].wait()
    loads["sp"].wait()
    dpart[...] = jnp.dot(act[...], dd_ref[...], preferred_element_type=F32).astype(BF)
    gpart[...] = lax.dot_general(
        sp_ref[...], act[...], (((1,), (1,)), ((), ())), preferred_element_type=F32
    )

    def tp_copies(gap):
        peer = at(me, (y + gap) % 4)
        return (
            remote(dpart, dland.at[gap - 1], tp_send.at[0, gap], tp_recv.at[0, gap], peer),
            remote(gpart, gland.at[gap - 1], tp_send.at[1, gap], tp_recv.at[1, gap], peer),
        )

    for gap in (2, 1, 3):
        for copy in tp_copies(gap):
            copy.start()


    kv_hop(1)
    w_arrived((0, 1))
    half_copy(1, 0, 0, right_x).start()
    w_arrived((0, 2))
    half_copy(2, 32, 1, left_x).start()
    w_spread_z(1)
    low_hop(0)

    def step_stage():
        loads["du"].wait()
        loads["db"].wait()
        for gap in (1, 3, 2):
            for copy in tp_copies(gap):
                copy.wait()
        gsum[...] = gpart[...] + gland[0] + gland[1] + gland[2]
        to_scalars = pltpu.make_async_copy(gsum, gates, load_sem.at[0])
        to_scalars.start()
        low = (
            dpart[...].astype(F32) + dland[0].astype(F32) + dland[1].astype(F32) + dland[2].astype(F32)
        ).astype(BF)
        for c in range(8):
            cols = slice(c * 256, (c + 1) * 256)
            raw = jnp.dot(low, du_ref[:, cols], preferred_element_type=F32) + db_ref[:, cols]
            size = jnp.maximum(raw, 0.0) + jnp.log1p(jnp.exp(-jnp.abs(raw)))
            drive = size * act[:, cols].astype(F32)
            for half in range(2):
                j = c * 2 + half
                steps[pl.ds(j, 128, stride=16), :] = size[:, half * 128:(half + 1) * 128]
                inject[pl.ds(j, 128, stride=16), :] = drive[:, half * 128:(half + 1) * 128]
        to_scalars.wait()

    def rows_of(t):
        return pl.ds(pl.multiple_of(t * 16, 16), 16)

    def first_pass(half):
        base = half * 8
        rates = [decay[(base + n) * 16:(base + n + 1) * 16, :] for n in range(8)]

        def advance(t, carried):
            size = steps[rows_of(t), :]
            drive = inject[rows_of(t), :]
            out = [
                jnp.exp2(rates[n] * size) * carried[n] + gates[base + n, t] * drive
                for n in range(8)
            ]
            return tuple(out) + (carried[8] + size,)

        zero = jnp.zeros((16, 128), F32)
        last = lax.fori_loop(0, 128, advance, (zero,) * 9, unroll=2)
        for n in range(8):
            ends[base + n, 0] = last[n].astype(BF)
            ends[base + n, 1] = last[8].astype(BF)

    def col_copies(gap):
        peer = col_peer(gap)
        return (
            remote(ends.at[(k + gap) % 16], ends_in.at[gap], col_send.at[gap], col_recv.at[gap], peer),
        )

    def col_start(gap, _):
        for copy in col_copies(gap):
            copy.start()
        return 0

    def col_wait(gap, _):
        for copy in col_copies(gap):
            copy.wait()
        return 0

    def ends_stage():
        lax.fori_loop(1, 16, col_start, 0)
        ends_in[0] = ends[k]

    def x_copy(gap):
        return remote(column, column_in.at[gap - 1], x_send.at[gap], x_recv.at[gap], x_peer(gap))

    def column_stage():
        lax.fori_loop(1, 16, col_wait, 0)
        my_rate = decay[rows_of(k), :]

        def chain(j, carried):
            state, sizes = carried
            before[j] = state
            shift[j] = sizes
            slot = (k + 16 - j) % 16
            size = ends_in[slot, 1].astype(F32)
            return (jnp.exp2(my_rate * size) * state + ends_in[slot, 0].astype(F32), sizes + size)

        zero = jnp.zeros((16, 128), F32)
        state, sizes = lax.fori_loop(0, 16, chain, (zero, zero))
        column[0] = state
        column[1] = sizes
        for gap in (2, 1, 3):
            x_copy(gap).start()

    def back_copy(gap):
        return remote(
            entry_out.at[(k + gap) % 16], entry.at[k], back_send.at[gap], back_recv.at[gap], col_peer(gap)
        )

    def back_arrival(gap):
        return remote(
            entry_out.at[(k + gap) % 16], entry.at[(k + 16 - gap) % 16],
            back_send.at[gap], back_recv.at[gap], col_peer(gap),
        )

    def back_start(gap, _):
        back_copy(gap).start()
        return 0

    def back_wait(gap, _):
        back_copy(gap).wait_send()
        back_arrival(gap).wait_recv()
        return 0

    def entry_stage():
        for gap in (1, 3, 2):
            x_copy(gap).wait()
        my_rate = decay[rows_of(k), :]
        incoming = jnp.zeros((16, 128), F32)
        for xs in range(3):
            slot = jnp.minimum((x + 3 - xs) % 4, 2)
            ahead = jnp.exp2(my_rate * column_in[slot, 1]) * incoming + column_in[slot, 0]
            incoming = jnp.where(xs < x, ahead, incoming)

        def finish(j, _):
            entry_out[j] = (before[j] + jnp.exp2(my_rate * shift[j]) * incoming).astype(BF)
            return 0

        lax.fori_loop(0, 16, finish, 0)
        lax.fori_loop(1, 16, back_start, 0)
        entry[k] = entry_out[k]

    def w_event(e):
        h = 1 + e // 4
        xs = e % 4
        w_arrived((2 * h - 1, xs))

        @pl.when((h < 3) | (xs < 2))
        def _():
            w_copy((2 * h - 1, xs), (2 * h + 1, xs), right_z).start()

        w_arrived((2 * h, xs))

        @pl.when(h < 3)
        def _():
            w_copy((2 * h, xs), (2 * h + 2, xs), left_z).start()

        @pl.when((h == 3) & (xs >= 2))
        def _():
            w_copy((2 * h, xs), (7, xs), left_z).start()

    def low_spread(zs, _):
        spread_x(2, zs)
        return 0

    def sweep(i, _):
        @pl.when(i == 1)
        def _():
            kv_hop(2)
            low_hop(1)
            w_spread_z(2)

        @pl.when(i == 2)
        def _():
            kv_hop(3)
            low_hop(2)
            half_copy(1, 0, 0, right_x).wait_recv()
            half_copy(2, 32, 1, left_x).wait_recv()
            w_spread_z(3)

        @pl.when(i == 3)
        def _():
            kv_hop(4)
            low_hop(3)

        for kind, near, peer in ((0, 1, right_x), (1, 2, left_x)):
            kv_arrived(kind, (1, i))
            kv_arrived(kind, (2, i))
            kv_copy(kind, (near, i), (3, i), peer).start()

        @pl.when(i == 6)
        def _():
            lax.fori_loop(0, 4, low_spread, 0)

        @pl.when(i == 7)
        def _():
            low_hop(4)
            lax.fori_loop(4, 8, low_spread, 0)

        @pl.when(i >= 2)
        def _():
            w_event(i - 2 + i // 7)

        attend_earlier(1, 2, i)

        @pl.when(i == 6)
        def _():
            w_event(5)

        @pl.when(i == 0)
        def _():
            step_stage()

        @pl.when(i == 1)
        def _():
            first_pass(0)

        @pl.when(i == 2)
        def _():
            first_pass(1)

        @pl.when(i == 3)
        def _():
            ends_stage()

        @pl.when(i > 0)
        def _():
            for kind in (0, 1):
                kv_arrived(kind, (3, i - 1))
            attend_earlier(0, 3, i - 1)

        @pl.when(i == 4)
        def _():
            column_stage()

        @pl.when(i == 6)
        def _():
            entry_stage()

        return 0

    lax.fori_loop(0, 8, sweep, 0)
    for kind in (0, 1):
        kv_arrived(kind, (3, 7))
    attend_earlier(0, 3, 7)

    inverse = 1.0 / l_ref[...]
    heads = []
    for h in range(4):
        pieces = []
        for r in range(2):
            cols = slice(r * 512 + h * 128, r * 512 + (h + 1) * 128)
            pieces.append((acc[:, cols] * inverse[:, cols]).astype(BF))
        heads.append(jnp.concatenate(pieces, axis=1))
    att[own_cols, :] = jnp.concatenate(heads, axis=0)
    att_swap = pair_copy(att.at[own_cols, :], att.at[own_cols, :], 3)
    att_swap.start()
    lax.fori_loop(1, 16, back_wait, 0)

    def second_pass(half):
        base = half * 8
        rates = [decay[(base + n) * 16:(base + n + 1) * 16, :] for n in range(8)]

        def advance(t, carried):
            size = steps[rows_of(t), :]
            drive = inject[rows_of(t), :]
            out = []
            mixed = scanned[rows_of(t), :] if half else None
            for n in range(8):
                state = jnp.exp2(rates[n] * size) * carried[n] + gates[base + n, t] * drive
                term = gates[NS + base + n, t] * state
                mixed = term if mixed is None else mixed + term
                out.append(state)
            scanned[rows_of(t), :] = mixed
            return tuple(out)

        lax.fori_loop(0, 128, advance, tuple(entry[base + n].astype(F32) for n in range(8)), unroll=2)

    def slot_of(gap):
        d = (y + gap + 4 - x) % 4
        return 2 * d - d // 2 - 4 * (d // 3)

    def y_copy(gap, r, g):
        first, count = GROUPS[g]
        rows = pl.ds(first, count)
        return remote(
            stage.at[slot_of(gap), r, rows], landed.at[gap, core, rows],
            y_send.at[gap, r, g], y_recv.at[gap, core, g], at(chip * 2 + r, (y + gap) % 4),
        )

    def y_arrival(gap, c, g):
        first, count = GROUPS[g]
        rows = pl.ds(first, count)
        return remote(
            stage.at[0, 0, rows], landed.at[gap, c, rows],
            y_send.at[gap, c, g], y_recv.at[gap, c, g], partner,
        )

    def project(g):
        first, count = GROUPS[g]
        for zs in range(first, first + count):
            part = jnp.dot(
                wbuf[zs].reshape(4 * (64 - LOW), 1024), att[...], preferred_element_type=F32
            ).astype(BF)
            for xs in range(4):
                for r in range(2):
                    stage[xs, r, zs] = part[xs * (64 - LOW):(xs + 1) * (64 - LOW), r * 128:(r + 1) * 128]
        for gap in (2, 1, 3):
            for r in range(2):
                y_copy(gap, r, g).start()
        y_copy_partner(g).start()
        for zs in range(first, first + count):
            landed[0, core, zs] = stage[slot_of(0), core, zs]

    def y_copy_partner(g):
        first, count = GROUPS[g]
        rows = pl.ds(first, count)
        return remote(
            stage.at[slot_of(0), other, rows], landed.at[0, core, rows],
            y_send.at[0, 0, g], y_recv.at[0, core, g], partner,
        )

    def low_cross(i, _):
        for zs, near, peer in ((2 * i, 1, right_x), (2 * i + 1, 2, left_x)):
            kv_arrived(2, (1, zs))
            kv_arrived(2, (2, zs))
            kv_copy(2, (near, zs), (3, zs), peer).start()
        return 0

    def y_low(gap, r):
        return remote(
            stage_low.at[slot_of(gap), r], landed_low.at[gap, core],
            y_send.at[gap, r, 5], y_recv.at[gap, core, 5], at(chip * 2 + r, (y + gap) % 4),
        )

    def y_low_partner():
        return remote(
            stage_low.at[slot_of(0), other], landed_low.at[0, core],
            y_send.at[0, 0, 5], y_recv.at[0, core, 5], partner,
        )

    def y_low_arrival(gap, c):
        return remote(
            stage_low.at[0, 0], landed_low.at[gap, c], y_send.at[gap, c, 5], y_recv.at[gap, c, 5], partner
        )

    def project_low():
        for zs in range(8):
            kv_arrived(2, (3, zs))
        for xs in range(4):
            part = jnp.dot(
                wlow[xs].reshape(8 * LOW, 1024), att[...], preferred_element_type=F32
            ).astype(BF)
            for r in range(2):
                stage_low[xs, r] = part[:, r * 128:(r + 1) * 128].reshape(8, LOW, 128)
        for gap in (2, 1, 3):
            for r in range(2):
                y_low(gap, r).start()
        y_low_partner().start()
        landed_low[0, core] = stage_low[slot_of(0), core]

    w_event(7)
    att_swap.wait()
    project(0)
    project(1)
    w_event(8)
    lax.fori_loop(0, 2, low_cross, 0)
    project(2)
    w_event(9)
    lax.fori_loop(2, 4, low_cross, 0)
    w_event(10)
    second_pass(0)
    w_event(11)
    project(3)
    project_low()
    for xs in range(4):
        w_arrived((7, xs))
    project(4)
    second_pass(1)
    loads["z"].wait()
    loads["sg"].wait()
    for j in range(16):
        cols = slice(j * 128, (j + 1) * 128)
        gate = z_ref[:, cols].astype(F32)
        mixed = scanned[pl.ds(j, 128, stride=16), :] + sg_ref[:, cols] * act[:, cols].astype(F32)
        mix_ref[:, cols] = (mixed * (gate / (1.0 + jnp.exp(-gate)))).astype(BF)

    for i in range(2):
        half_copy(i + 1, 32 * i, i, right_x).wait_send()
    w_copy((0, 0), (0, 1), right_x).wait_send()
    w_copy((0, 0), (0, 2), left_x).wait_send()

    def drain(zs, _):
        for kind in (0, 1, 2):
            @pl.when((zs > 0) & (zs < 7))
            def _():
                kv_copy(kind, (0, zs), (0, zs), right_z).wait_send()

            for xs in range(1, 4):
                kv_copy(kind, (xs, zs), (xs, zs), right_z).wait_send()

        @pl.when(zs > 0)
        def _():
            for xs in range(4):
                w_copy((zs, xs), (zs, xs), right_z).wait_send()

        return 0

    lax.fori_loop(0, 8, drain, 0)
    for kind in (0, 1, 2):
        kv_copy(kind, (0, 7), (0, 7), right_z).wait_send()
    loads["res"].wait()
    for g in range(5):
        y_copy_partner(g).wait_send()
        for gap in (1, 2, 3):
            for r in range(2):
                y_copy(gap, r, g).wait_send()
        y_arrival(0, other, g).wait_recv()
        for gap in (1, 3, 2):
            for c in range(2):
                y_arrival(gap, c, g).wait_recv()
        first, count = GROUPS[g]
        for zs in range(first, first + count):
            for c in range(2):
                part = landed[0, c, zs].astype(F32)
                for gap in range(1, 4):
                    part = part + landed[gap, c, zs].astype(F32)
                rows = pl.ds(pl.multiple_of(z_of(zs) * 128 + c * 64 + LOW, LOW), 64 - LOW)
                out_t[rows, :] = part
    y_low_partner().wait_send()
    for gap in (1, 2, 3):
        for r in range(2):
            y_low(gap, r).wait_send()
    y_low_arrival(0, other).wait_recv()
    for gap in (1, 3, 2):
        for c in range(2):
            y_low_arrival(gap, c).wait_recv()
    for zs in range(8):
        for c in range(2):
            part = landed_low[0, c, zs].astype(F32)
            for gap in range(1, 4):
                part = part + landed_low[gap, c, zs].astype(F32)
            rows = pl.ds(pl.multiple_of(z_of(zs) * 128 + c * 64, 64), LOW)
            out_t[rows, :] = part
    for zo in range(8):
        cols = slice(zo * 128, (zo + 1) * 128)
        out_ref[:, cols] = (res_ref[:, cols].astype(F32) + out_t[cols, :].T).astype(BF)


def block(
    x_stream, z_stream, conv_kernel, conv_bias, delta_down, state_proj, delta_up, delta_bias,
    log_decay, skip_gain, queries, key_heads, values, out_proj, residual,
):
    dma = pltpu.SemaphoreType.DMA
    operands = (
        x_stream, z_stream, conv_kernel, conv_bias[None, :], delta_down, state_proj, delta_up,
        delta_bias[None, :], log_decay, skip_gain[None, :], queries, key_heads, values, out_proj.T, residual,
    )
    copies = [pltpu.VMEM(a.shape, a.dtype) for i, a in enumerate(operands) if i != 13]
    states = pltpu.VMEM((16, 16, 128), F32)
    by_token = pltpu.VMEM((2048, 128), F32)
    return pl.pallas_call(
        block_kernel,
        out_shape=(
            jax.ShapeDtypeStruct(x_stream.shape, BF), jax.ShapeDtypeStruct(residual.shape, BF)
        ),
        in_specs=[pl.BlockSpec(memory_space=pl.ANY)] * 15,
        out_specs=(pl.BlockSpec(memory_space=pltpu.VMEM),) * 2,
        scratch_shapes=copies + [
            pltpu.VMEM((2, 128, 512), BF),
            pltpu.VMEM((256, 128), BF),
            pltpu.VMEM((128, 1024), BF),
            pltpu.VMEM((4, 8, 256, 128), BF),
            pltpu.VMEM((4, 8, 128, 256), BF),
            pltpu.VMEM((4, 8, LOW, 1024), BF),
            pltpu.VMEM((8, 4, 64 - LOW, 1024), BF),
            pltpu.VMEM((1, 1024), F32),
            pltpu.VMEM((1, 1024), F32),
            pltpu.VMEM((128, 1024), F32),
            pltpu.VMEM((1024, 256), BF),
            pltpu.VMEM((4, 2, 8, 64 - LOW, 128), BF),
            pltpu.VMEM((4, 2, 8, 64 - LOW, 128), BF),
            pltpu.VMEM((4, 2, 8, LOW, 128), BF),
            pltpu.VMEM((4, 2, 8, LOW, 128), BF),
            pltpu.VMEM((1024, 128), F32),
            pltpu.VMEM((16, 2048), BF),
            pltpu.VMEM((136, 2048), F32),
            pltpu.VMEM((128, 2048), BF),
            pltpu.VMEM((128, 256), BF),
            pltpu.VMEM((32, 128), F32),
            pltpu.VMEM((3, 128, 256), BF),
            pltpu.VMEM((3, 32, 128), F32),
            pltpu.VMEM((32, 128), F32),
            pltpu.SMEM((32, 128), F32),
            by_token, by_token, by_token,
            pltpu.VMEM((256, 128), F32),
            pltpu.VMEM((16, 2, 16, 128), BF),
            pltpu.VMEM((16, 2, 16, 128), BF),
            states, states,
            pltpu.VMEM((2, 16, 128), F32),
            pltpu.VMEM((3, 2, 16, 128), F32),
            pltpu.VMEM((16, 16, 128), BF),
            pltpu.VMEM((16, 16, 128), BF),
            dma((16,)), dma((4,)), dma((4,)), dma((3, 4, 8)), dma((3, 4, 8)), dma((8, 4)), dma((8, 4)),
            dma((2,)), dma((2,)), dma((4, 2, 6)), dma((4, 2, 6)), dma((1,)), dma((1,)),
            dma((2, 4)), dma((2, 4)), dma((16,)), dma((16,)), dma((4,)), dma((4,)),
            dma((16,)), dma((16,)),
        ],
        compiler_params=pltpu.CompilerParams(
            collective_id=0, has_side_effects=True, vmem_limit_bytes=56 * 1024 * 1024
        ),
    )(*operands)


def solution(mesh):
    both = P("ctx", "tp")
    placed = (
        both, both, P(None, "tp"), P("tp"), P("tp", None), P(None, "tp"), P(None, "tp"), P("tp"),
        P(None, "tp"), P("tp"), both, both, both, P("tp", "ctx"), both,
    )
    return jax.shard_map(
        block, mesh=mesh, in_specs=placed, out_specs=(both, both), check_vma=False
    )
```
